32 devices in a mesh: seq: 4 (over y, x), tensor: 8 (over z, core).
Axes of the slice: x: 2, y: 2, z: 4, core: 2. Of those that a mesh axis runs over, the one named last changes fastest.
Arguments:
- frames: bfloat16 [2048, 8192], P('seq', 'tensor'), may hold values from -6 to 6
- up_factors: bfloat16 [6, 128, 256, 256], P(None, 'tensor'), may hold values from -0.15625 to 0.15625
- down_factors: bfloat16 [6, 128, 256, 256], P(None, 'tensor'), may hold values from -0.078125 to 0.078125
- pattern: int32 [128, 5], P('tensor'), may hold values 0 or 1
- level_bits: int32 [5], replicated, may hold values from 0 to 4, each once
- taps: float32 [3, 8192], P(None, 'tensor'), may hold values from -3 to 3
- cotangent: bfloat16 [2048, 8192], P('seq', 'tensor'), may hold values from -6 to 6
Outputs:
- convolved: bfloat16 [2048, 8192], P('seq', 'tensor')
- grad_frames: bfloat16 [2048, 8192], P('seq', 'tensor')
- grad_up: float32 [6, 128, 256, 256], P(None, 'tensor', 'seq')
- grad_down: float32 [6, 128, 256, 256], P(None, 'tensor', 'seq')
The draws below stay inside these ranges and needn't reach their ends.
Inputs may be any that keep to these rules, and one draw needn't show every extreme that they name: Level l pairs feature block i with block i xor 2^level_bits[l]; each of 0..4 appears once.
All inputs are finite; a program needn't handle non-finite values. No bound on the sum of `pattern` on one device may be relied on, other than what follows from the above.
Results may differ from the reference program's by a relative error of at most 0.012.
Values may be sent and summed in bfloat16 or wider, within the bound.
No kernel may reach another device: no remote copies, remote signals or barrier semaphores. Data moves between devices by JAX's collectives and lax.ppermute only.
A program may use at most 192 MiB of HBM per device.

```python
import jax
import jax.numpy as jnp
from jax import lax

D = 8192
H = 32768
BS = 256
LEVELS = 5
FRAMES_DEV = 512
FRAMES = 2048
NHB = 128
N_SEQ = 4


def set_ends(entries, stream_key, least, largest):
    index_at = [jax.random.randint(jax.random.fold_in(stream_key, axis), (), 0, length) for axis, length in enumerate(entries.shape)]
    main_axis = entries.shape.index(max(entries.shape))
    beside = index_at[:main_axis] + [(index_at[main_axis] + 1) % entries.shape[main_axis]] + index_at[main_axis + 1:]
    return entries.at[tuple(index_at)].set(least).at[tuple(beside)].set(largest)


def block_levels(own_key, shape, shards, smallest, largest):
    def one(axis_at, blocks):
        heights = jax.random.uniform(jax.random.fold_in(jax.random.fold_in(own_key, 6), axis_at), (blocks,), jnp.float32, smallest / len(shards), largest / len(shards))
        return jnp.repeat(jnp.exp(heights), shape[axis_at] // blocks).reshape((-1,) + (1,) * (len(shape) - axis_at - 1))

    loudness = one(*shards[0])
    for cut in shards[1:]:
        loudness = loudness * one(*cut)
    return loudness


def scatter_about(stream_key, extent, scale, reach, shards=(), kind=jnp.bfloat16):
    drawn = scale * jax.random.normal(stream_key, extent, jnp.float32)
    if shards:
        drawn = drawn * block_levels(stream_key, extent, shards, -0.22, 0.18)
    return jnp.clip(drawn, -reach, reach).astype(kind)


def setup_inputs(seed: int = 0) -> dict:
    splits = jax.random.split(jax.random.key(seed), 8)
    frames = scatter_about(splits[0], (FRAMES, D), 1.0, 6.0, ((0, 4), (1, 8)))
    up_factors = scatter_about(splits[1], (LEVELS + 1, NHB, BS, BS), ((LEVELS + 1) * BS) ** -0.5, 0.15625, ((1, 8),))
    down_factors = scatter_about(splits[2], (LEVELS + 1, NHB, BS, BS), ((LEVELS + 1) * (H // D) * BS) ** -0.5, 0.078125, ((1, 8),))
    pattern = set_ends((jax.random.randint(splits[3], (NHB, LEVELS), 0, 4) < 3).astype(jnp.int32), jax.random.fold_in(splits[3], 1), 0, 1)
    level_bits = jax.random.permutation(splits[4], LEVELS).astype(jnp.int32)
    taps = scatter_about(splits[5], (3, D), 0.6, 3.0, ((1, 8),), jnp.float32)
    cotangent = scatter_about(splits[6], (FRAMES, D), 1.0, 6.0, ((0, 4), (1, 8)))
    return {"frames": frames, "up_factors": up_factors, "down_factors": down_factors, "pattern": pattern, "level_bits": level_bits, "taps": taps, "cotangent": cotangent}


coef = 0.7978845608028654

def gelu_value(u):
    return 0.5 * u * (1.0 + jnp.tanh(coef * (u + 0.044715 * u * u * u)))

def gelu_slope(u):
    inner = jnp.tanh(coef * (u + 0.044715 * u * u * u))
    return 0.5 * (1.0 + inner) + 0.5 * u * (1.0 - inner * inner) * coef * (1.0 + 3.0 * 0.044715 * u * u)

def reference(frames, up_factors, down_factors, pattern, level_bits, taps, cotangent):
    f32 = jnp.float32
    nblocks = D // BS
    ratio = H // D
    upf = up_factors.reshape(LEVELS + 1, nblocks, ratio, BS, BS)
    downf = down_factors.reshape(LEVELS + 1, nblocks, ratio, BS, BS)
    masks = pattern.reshape(nblocks, ratio, LEVELS).astype(f32)
    blocks = jnp.arange(nblocks, dtype=jnp.int32)
    partners = [jnp.bitwise_xor(blocks, jnp.left_shift(jnp.int32(1), level_bits[lev]).astype(jnp.int32)) for lev in range(LEVELS)]
    inputs = frames.reshape(FRAMES, nblocks, BS).astype(f32)
    pre = jnp.einsum('rbs,bhsf->rbhf', inputs, upf[0].astype(f32))
    for lev in range(LEVELS):
        moved = inputs[:, partners[lev]]
        pre = pre + masks[None, :, :, lev, None] * jnp.einsum('rbs,bhsf->rbhf', moved, upf[lev + 1].astype(f32))
    hidden = gelu_value(pre).astype(jnp.bfloat16)
    hidf = hidden.astype(f32)
    mixed = jnp.einsum('rbhf,bhfs->rbs', hidf, downf[0].astype(f32))
    for lev in range(LEVELS):
        masked = (hidden * masks[None, :, :, lev, None].astype(jnp.bfloat16)).astype(f32)
        part = jnp.einsum('rbhf,bhfs->rbs', masked, downf[lev + 1].astype(f32))
        mixed = mixed + part[:, partners[lev]]
    mixed = mixed.reshape(FRAMES, D).astype(jnp.bfloat16)
    padded = jnp.pad(mixed.astype(f32), ((1, 1), (0, 0)))
    convolved = (taps[0] * padded[:-2] + taps[1] * padded[1:-1] + taps[2] * padded[2:]).astype(jnp.bfloat16)
    gpad = jnp.pad(cotangent.astype(f32), ((1, 1), (0, 0)))
    grad_mixed = (taps[0] * gpad[2:] + taps[1] * gpad[1:-1] + taps[2] * gpad[:-2]).astype(jnp.bfloat16)
    gmix = grad_mixed.reshape(FRAMES, nblocks, BS).astype(f32)
    grad_hidden = jnp.einsum('rbs,bhfs->rbhf', gmix, downf[0].astype(f32))
    for lev in range(LEVELS):
        moved = gmix[:, partners[lev]]
        grad_hidden = grad_hidden + masks[None, :, :, lev, None] * jnp.einsum('rbs,bhfs->rbhf', moved, downf[lev + 1].astype(f32))
    grad_pre = (grad_hidden * gelu_slope(pre)).astype(jnp.bfloat16)
    gpre = grad_pre.astype(f32)
    grad_in = jnp.einsum('rbhf,bhsf->rbs', gpre, upf[0].astype(f32))
    for lev in range(LEVELS):
        masked = (grad_pre * masks[None, :, :, lev, None].astype(jnp.bfloat16)).astype(f32)
        part = jnp.einsum('rbhf,bhsf->rbs', masked, upf[lev + 1].astype(f32))
        grad_in = grad_in + part[:, partners[lev]]
    grad_frames = grad_in.reshape(FRAMES, D).astype(jnp.bfloat16)
    scale = 1.0 / jnp.sqrt(jnp.asarray(FRAMES, f32))

    def group_sum(left, right):
        left_q = left.reshape(N_SEQ, FRAMES_DEV, nblocks, -1)
        right_q = right.reshape(N_SEQ, FRAMES_DEV, nblocks, ratio, BS)
        return (left_q, right_q)

    def reduce_terms(terms):
        rounded = (terms * scale).astype(jnp.bfloat16)
        rounded = lax.optimization_barrier(rounded)
        return lax.optimization_barrier(jnp.sum(rounded.astype(f32), axis=0))
    up_list = []
    down_list = []
    for lev in range(LEVELS + 1):
        if lev == 0:
            inp_l = inputs
            gm_l = gmix
            weight = jnp.ones((nblocks, ratio), f32)
        else:
            inp_l = inputs[:, partners[lev - 1]]
            gm_l = gmix[:, partners[lev - 1]]
            weight = masks[:, :, lev - 1]
        left_q, right_q = group_sum(inp_l, gpre)
        terms = jnp.einsum('qrbs,qrbhf->qbhsf', left_q, right_q) * weight[None, :, :, None, None]
        up_list.append(reduce_terms(terms))
        hid_q = hidf.reshape(N_SEQ, FRAMES_DEV, nblocks, ratio, BS)
        gm_q = gm_l.reshape(N_SEQ, FRAMES_DEV, nblocks, BS)
        terms = jnp.einsum('qrbhf,qrbs->qbhfs', hid_q, gm_q) * weight[None, :, :, None, None]
        down_list.append(reduce_terms(terms))
    grad_up = jnp.stack(up_list).reshape(LEVELS + 1, H // BS, BS, BS)
    grad_down = jnp.stack(down_list).reshape(LEVELS + 1, H // BS, BS, BS)
    return (convolved, grad_frames, grad_up, grad_down)
```

```python
import functools
import math

import jax
import jax.numpy as jnp
from jax import lax
from jax.experimental import pallas as pl
from jax.experimental.pallas import tpu as pltpu
from jax.sharding import PartitionSpec as P

coef = 0.7978845608028654
cubic = 0.044715
f32 = jnp.float32
bf16 = jnp.bfloat16
VMEM_LIMIT = 56 * 1024 * 1024
ANY = pl.BlockSpec(memory_space=pl.ANY)


def swapped(array, axis, bit):
    return lax.ppermute(array, axis, [(i, i ^ 1 << bit) for i in range(lax.axis_size(axis))])


def after(value, *others):
    return lax.optimization_barrier((value,) + others)[0]


def cost(flops, moved, transcendentals=0):
    return pl.CostEstimate(flops=flops, bytes_accessed=moved, transcendentals=transcendentals)


def halo(array):
    peers = lax.axis_size("seq")
    up = [(i, i + 1) for i in range(peers - 1)]
    down = [(i + 1, i) for i in range(peers - 1)]
    rows = array.shape[0]
    before = lax.ppermute(lax.slice_in_dim(array, rows - 1, rows), "seq", up)
    behind = lax.ppermute(lax.slice_in_dim(array, 0, 1), "seq", down)
    return before, behind


def convolution_kernel(x_ref, before_ref, behind_ref, taps_ref, out_ref, *, order, blocked):
    x = x_ref[...].astype(f32)
    rows = x.shape[0]
    at = lax.broadcasted_iota(jnp.int32, x.shape, 0)
    earlier = jnp.where(at == 0, before_ref[...].astype(f32), pltpu.roll(x, 1, 0))
    later = jnp.where(at == rows - 1, behind_ref[...].astype(f32), pltpu.roll(x, rows - 1, 0))
    first, middle, last = order
    out = (
        taps_ref[first : first + 1, :] * earlier
        + taps_ref[middle : middle + 1, :] * x
        + taps_ref[last : last + 1, :] * later
    ).astype(bf16)
    if blocked:
        out_ref[0] = out
    else:
        out_ref[...] = out


def convolution(x, before, behind, taps, order, width, blocked):
    rows, local = x.shape
    column = lambda r: pl.BlockSpec((r, width), lambda i: (0, i))
    if blocked:
        shape = jax.ShapeDtypeStruct((local // width, rows, width), bf16)
        out_spec = pl.BlockSpec((1, rows, width), lambda i: (i, 0, 0))
    else:
        shape = jax.ShapeDtypeStruct((rows, local), bf16)
        out_spec = column(rows)
    return pl.pallas_call(
        functools.partial(convolution_kernel, order=order, blocked=blocked),
        out_shape=shape,
        grid=(local // width,),
        in_specs=[column(rows), column(1), column(1), column(3)],
        out_specs=out_spec,
        compiler_params=pltpu.CompilerParams(vmem_limit_bytes=VMEM_LIMIT),
        cost_estimate=cost(10 * rows * local, 4 * rows * local),
        name="convolution",
    )(x, before, behind, taps)


def layer_kernel(
    level_bits, pattern, place, *refs, first, ratio, levels, local_bits, remote_bits, peers, scale
):
    terms = 1 + levels
    x_refs, refs = refs[:terms], refs[terms:]
    g_refs, refs = refs[:terms], refs[terms:]
    u_ref, d_ref = refs[:2]
    sends = refs[2:6]
    home_ref = refs[6]
    away_refs = refs[7 : 7 + remote_bits]
    x_all, x_turned, g_all, u_all, d_all, h_all, p_all, turned = refs[7 + remote_bits :]
    jj, h = pl.program_id(0), pl.program_id(1)
    rows, width = x_refs[0].shape[1:]
    slab = width // peers
    k = (first + jj) * ratio + h
    me = place[0]
    stages = peers.bit_length() - 1

    level_at, present = [], []
    for bit in range(levels):
        at = jnp.int32(0)
        for level in range(levels):
            at = at + jnp.where(level_bits[level] == bit, level, 0)
        level_at.append(at + 1)
        present.append(pattern[k, at])

    def rearranged(target, base):
        for r in range(peers):
            start = pl.multiple_of((me ^ r) * slab, slab)
            target[base + r * slab : base + (r + 1) * slab, :] = turned[pl.ds(start, slab), :]

    @pl.when(h == 0)
    def _():
        for b in range(terms):
            block = x_refs[b][0]
            x_all[:, b * width : (b + 1) * width] = block
            g_all[:, b * width : (b + 1) * width] = g_refs[b][0]
            turned[...] = block.T
            rearranged(x_turned, b * width)

    wide = pl.ds(pl.multiple_of(h * width, width), width)
    for b in range(terms):
        if b == 0:
            u, d = u_ref[0, 0], d_ref[0, 0]
        else:
            mask = present[b - 1].astype(f32).astype(bf16)
            u, d = u_ref[level_at[b - 1], 0] * mask, d_ref[level_at[b - 1], 0] * mask
        u_all[h, b * width : (b + 1) * width, :] = u
        d_all[wide, b * width : (b + 1) * width] = d

    pre = jnp.dot(x_all[...], u_all[h], preferred_element_type=f32)
    square = pre * pre
    inner = jnp.tanh(coef * (pre + cubic * (square * pre)))
    half = 0.5 * (1.0 + inner)
    slope = half + (0.5 * coef) * pre * (1.0 - inner * inner) * (1.0 + (3.0 * cubic) * square)
    hidden = (pre * half).astype(bf16)
    h_all[h] = hidden
    turned[...] = hidden.T
    hidden_turned = jnp.concatenate(
        [
            turned[pl.ds(pl.multiple_of((me ^ r) * slab, slab), slab), :]
            for r in range(peers)
        ],
        axis=0,
    )
    grad_hidden = lax.dot_general(
        g_all[...], d_all[wide, :], (((1,), (1,)), ((), ())), preferred_element_type=f32
    )
    grad_pre = (grad_hidden * slope).astype(bf16)
    p_all[h] = grad_pre

    for b in range(terms):
        span = slice(b * width, (b + 1) * width)
        up = jnp.dot(x_turned[span, :], grad_pre, preferred_element_type=f32)
        down = jnp.dot(hidden_turned, g_all[:, span], preferred_element_type=f32)
        if b == 0:
            factor, slot = scale, 0
        else:
            factor, slot = present[b - 1].astype(f32) * scale, level_at[b - 1]
        up, down = (up * factor).astype(bf16), (down * factor).astype(bf16)
        for value, sent, kept, bit in ((up, sends[0], sends[1], 0), (down, sends[2], sends[3], stages - 1)):
            counts = [0, 0]
            for r in range(peers):
                which = r >> bit & 1
                target = sent if which else kept
                target[counts[which], slot, 0] = value[r * slab : (r + 1) * slab, :]
                counts[which] += 1

    @pl.when(h == ratio - 1)
    def _():
        for b in range(terms):
            span = slice(b * width, (b + 1) * width)
            for side in range(2):
                total = None
                for other in range(ratio):
                    if side == 0:
                        part = jnp.dot(
                            h_all[other],
                            d_all[other * width : (other + 1) * width, span],
                            preferred_element_type=f32,
                        )
                    else:
                        part = lax.dot_general(
                            p_all[other],
                            u_all[other, span, :],
                            (((1,), (1,)), ((), ())),
                            preferred_element_type=f32,
                        )
                    total = part if total is None else total + part
                total = total.astype(bf16)
                if b <= local_bits:
                    home_ref[side, b, 0] = total
                else:
                    away_refs[b - 1 - local_bits][side, 0] = total


def layer(level_bits, pattern, place, x_home, g_home, x_away, g_away, up_factors, down_factors, first, count, peers, scale):
    terms, hidden_dev, width, _ = up_factors.shape
    levels = terms - 1
    blocks_dev, rows, _ = x_home.shape
    ratio = hidden_dev // blocks_dev
    local_bits = blocks_dev.bit_length() - 1
    remote_bits = levels - local_bits
    slab = width // peers
    home = [
        pl.BlockSpec((1, rows, width), lambda j, h, *s, flip=flip: ((first + j) ^ flip, 0, 0))
        for flip in [0] + [1 << bit for bit in range(local_bits)]
    ]
    away = [pl.BlockSpec((1, rows, width), lambda j, h, *s: (j, 0, 0))] * remote_bits
    weight = pl.BlockSpec((terms, 1, width, width), lambda j, h, *s: (0, (first + j) * ratio + h, 0, 0))
    piece = pl.BlockSpec((peers // 2, terms, 1, slab, width), lambda j, h, *s: (0, 0, j * ratio + h, 0, 0))
    piece_shape = jax.ShapeDtypeStruct((peers // 2, terms, count * ratio, slab, width), bf16)
    home_out = pl.BlockSpec((2, 1 + local_bits, 1, rows, width), lambda j, h, *s: (0, 0, j, 0, 0))
    away_out = pl.BlockSpec((2, 1, rows, width), lambda j, h, *s: (0, j, 0, 0))
    steps = count * ratio
    outs = pl.pallas_call(
        functools.partial(
            layer_kernel,
            first=first,
            ratio=ratio,
            levels=levels,
            local_bits=local_bits,
            remote_bits=remote_bits,
            peers=peers,
            scale=scale,
        ),
        out_shape=[piece_shape] * 4
        + [jax.ShapeDtypeStruct((2, 1 + local_bits, count, rows, width), bf16)]
        + [jax.ShapeDtypeStruct((2, count, rows, width), bf16)] * remote_bits,
        grid_spec=pltpu.PrefetchScalarGridSpec(
            num_scalar_prefetch=3,
            grid=(count, ratio),
            in_specs=home + away + home + away + [weight] * 2,
            out_specs=[piece] * 4 + [home_out] + [away_out] * remote_bits,
            scratch_shapes=[
                pltpu.VMEM((rows, terms * width), bf16),
                pltpu.VMEM((terms * width, rows), bf16),
                pltpu.VMEM((rows, terms * width), bf16),
                pltpu.VMEM((ratio, terms * width, width), bf16),
                pltpu.VMEM((ratio * width, terms * width), bf16),
                pltpu.VMEM((ratio, rows, width), bf16),
                pltpu.VMEM((ratio, rows, width), bf16),
                pltpu.VMEM((width, rows), bf16),
            ],
        ),
        compiler_params=pltpu.CompilerParams(vmem_limit_bytes=VMEM_LIMIT),
        cost_estimate=cost(
            12 * steps * terms * rows * width * width,
            2 * steps * terms * width * width * 4 + 8 * count * terms * rows * width,
            steps * rows * width,
        ),
        name="layer",
    )(
        level_bits, pattern, place,
        *[x_home] * len(home), *x_away, *[g_home] * len(home), *g_away, up_factors, down_factors,
    )
    return outs[:4], outs[4], outs[5:]


def pair_kernel(kept_ref, got_ref, next_sent_ref, next_kept_ref, *, bit):
    counts = [0, 0]
    for r in range(kept_ref.shape[0]):
        which = r >> bit & 1
        total = (kept_ref[r].astype(f32) + got_ref[r].astype(f32)).astype(bf16)
        target = next_sent_ref if which else next_kept_ref
        target[counts[which]] = total
        counts[which] += 1


def pair_sum(kept, got, bit):
    parts, terms, blocks, slab, width = kept.shape
    spec = lambda n: pl.BlockSpec((n, 1, blocks, slab, width), lambda i: (0, i, 0, 0, 0))
    half = jax.ShapeDtypeStruct((parts // 2, terms, blocks, slab, width), bf16)
    return pl.pallas_call(
        functools.partial(pair_kernel, bit=bit),
        out_shape=[half, half],
        grid=(terms,),
        in_specs=[spec(parts)] * 2,
        out_specs=[spec(parts // 2)] * 2,
        compiler_params=pltpu.CompilerParams(vmem_limit_bytes=VMEM_LIMIT),
        cost_estimate=cost(kept.size, 6 * kept.size),
        name="pair_sum",
    )(kept, got)


def finish_kernel(a_kept, a_got, b_kept, b_got, *refs):
    a_out, b_out = refs[-2:]
    a_out[...] = a_kept[0].astype(f32) + a_got[0].astype(f32)
    b_out[...] = b_kept[0].astype(f32) + b_got[0].astype(f32)


def finish(a_kept, a_got, b_kept, b_got, outs, first, hidden_dev):
    _, terms, blocks, slab, width = a_kept.shape
    spec = pl.BlockSpec((1, terms, 1, slab, width), lambda i: (0, 0, i, 0, 0))
    out_spec = pl.BlockSpec((terms, 1, slab, width), lambda i: (0, first + i, 0, 0))
    shape = jax.ShapeDtypeStruct((terms, hidden_dev, slab, width), f32)
    extra = [] if outs is None else list(outs)
    return pl.pallas_call(
        finish_kernel,
        out_shape=[shape, shape],
        grid=(blocks,),
        in_specs=[spec] * 4 + [ANY] * len(extra),
        out_specs=[out_spec] * 2,
        input_output_aliases={4 + i: i for i in range(len(extra))},
        compiler_params=pltpu.CompilerParams(vmem_limit_bytes=VMEM_LIMIT),
        cost_estimate=cost(2 * a_kept.size, 16 * a_kept.size),
        name="finish",
    )(a_kept, a_got, b_kept, b_got, *extra)


def combine_kernel(*refs, sizes, remote_bits, local_bits, blocks_dev):
    homes, refs = refs[: len(sizes)], refs[len(sizes) :]
    aways, (mixed_ref, grad_ref) = refs[:-2], refs[-2:]
    where = [(g, i) for g, size in enumerate(sizes) for i in range(size)]
    width = homes[0].shape[-1]
    for j in range(blocks_dev):
        for side, target in ((0, mixed_ref), (1, grad_ref)):
            g, i = where[j]
            total = homes[g][side, 0, i].astype(f32)
            for bit in range(local_bits):
                g, i = where[j ^ 1 << bit]
                total = total + homes[g][side, 1 + bit, i].astype(f32)
            g, i = where[j]
            for bit in range(remote_bits):
                total = total + aways[g * remote_bits + bit][side, i].astype(f32)
            target[:, j * width : (j + 1) * width] = total.astype(bf16)


def combine(homes, aways, sizes, blocks_dev):
    rows, width = homes[0].shape[-2:]
    local_bits, remote_bits = homes[0].shape[1] - 1, len(aways[0])
    chunk = min(rows, 128)
    home = [pl.BlockSpec((2, 1 + local_bits, n, chunk, width), lambda i: (0, 0, 0, i, 0)) for n in sizes]
    away = [pl.BlockSpec((2, n, chunk, width), lambda i: (0, 0, i, 0)) for n in sizes for _ in range(remote_bits)]
    out = pl.BlockSpec((chunk, blocks_dev * width), lambda i: (i, 0))
    shape = jax.ShapeDtypeStruct((rows, blocks_dev * width), bf16)
    return pl.pallas_call(
        functools.partial(
            combine_kernel, sizes=sizes, remote_bits=remote_bits, local_bits=local_bits, blocks_dev=blocks_dev
        ),
        out_shape=[shape, shape],
        grid=(rows // chunk,),
        in_specs=home + away,
        out_specs=[out, out],
        compiler_params=pltpu.CompilerParams(vmem_limit_bytes=VMEM_LIMIT),
        cost_estimate=cost(12 * shape.size, 28 * shape.size),
        name="combine",
    )(*homes, *[part for group in aways for part in group])


def local(frames, up_factors, down_factors, pattern, level_bits, taps, cotangent):
    rows, local_width = frames.shape
    terms, hidden_dev, width, _ = up_factors.shape
    blocks_dev = local_width // width
    ratio = hidden_dev // blocks_dev
    levels = terms - 1
    local_bits = blocks_dev.bit_length() - 1
    remote_bits = levels - local_bits
    peers = lax.axis_size("seq")
    stages = peers.bit_length() - 1
    scale = 1.0 / math.sqrt(rows * peers)
    place = lax.axis_index("seq").astype(jnp.int32).reshape(1)
    sizes = [1] * blocks_dev
    starts = [sum(sizes[:g]) for g in range(len(sizes))]
    bits = range(remote_bits)

    before, behind = halo(cotangent)
    x_home = frames.reshape(rows, blocks_dev, width).transpose(1, 0, 2)

    def fetch(pieces):
        return [swapped(piece, "tensor", bit) for bit, piece in zip(bits, pieces)]

    x_first = x_home[: sizes[0]]
    x_away = [fetch([x_first] * remote_bits)]
    g_home = convolution(cotangent, before, behind, taps, (2, 1, 0), width, True)
    g_away = [fetch([g_home[: sizes[0]]] * remote_bits)]

    grads, homes, aways = [], [], []
    outs = None
    pending = []

    def start_sums(pieces):
        up_sent, up_kept, down_sent, down_kept = pieces
        return {
            "up": (up_kept, swapped(up_sent, "seq", 0)),
            "down": (down_kept, swapped(down_sent, "seq", stages - 1)),
            "done": 1,
        }

    def next_sums(state, behind_value):
        stage = state["done"]
        order_up = list(range(stages))
        order_down = order_up[::-1]
        result = {"done": stage + 1}
        for name, order in (("up", order_up), ("down", order_down)):
            kept, got = state[name]
            if behind_value is not None:
                got = after(got, behind_value)
            remaining = [bit for bit in range(stages) if bit not in order[:stage]]
            sent, kept = pair_sum(kept, got, remaining.index(order[stage]))
            result[name] = (kept, swapped(sent, "seq", order[stage]))
        return result

    for g, (first, size) in enumerate(zip(starts, sizes)):
        if g + 1 < len(sizes):
            nxt = slice(starts[g + 1], starts[g + 1] + sizes[g + 1])
            both = jnp.stack([x_home[nxt], g_home[nxt]])
            tied = [after(both, x_away[g][bit], g_away[g][bit]) for bit in bits]
            arrived = fetch(tied)
            x_away.append([value[0] for value in arrived])
            g_away.append([value[1] for value in arrived])
        pieces, home, away = layer(
            level_bits, pattern, place, x_home, g_home, x_away[g], g_away[g],
            up_factors, down_factors, first, size, peers, scale,
        )
        homes.append(home)
        state = start_sums(pieces)
        aways.append(fetch(away))
        for index, older in enumerate(pending):
            if older["done"] < stages:
                pending[index] = next_sums(older, home)
        pending.append(state)

    while any(state["done"] < stages for state in pending):
        for index, older in enumerate(pending):
            if older["done"] < stages:
                pending[index] = next_sums(older, None)
    mixed, grad_frames = combine(homes, aways, sizes, blocks_dev)
    before, behind = halo(mixed)
    convolved = convolution(mixed, before, behind, taps, (0, 1, 2), width, False)
    for state, first in zip(pending, starts):
        outs = finish(*state["up"], *state["down"], outs, first * ratio, hidden_dev)
    return convolved, grad_frames, outs[0], outs[1]


def solution(mesh):
    in_specs = (
        P("seq", "tensor"),
        P(None, "tensor", None, None),
        P(None, "tensor", None, None),
        P("tensor", None),
        P(),
        P(None, "tensor"),
        P("seq", "tensor"),
    )
    out_specs = (
        P("seq", "tensor"),
        P("seq", "tensor"),
        P(None, "tensor", "seq", None),
        P(None, "tensor", "seq", None),
    )
    return jax.shard_map(local, mesh=mesh, in_specs=in_specs, out_specs=out_specs, check_vma=False)
```

```python
import functools
import math

import jax
import jax.numpy as jnp
from jax import lax
from jax.experimental import pallas as pl
from jax.experimental.pallas import tpu as pltpu
from jax.sharding import PartitionSpec as P

coef = 0.7978845608028654
cubic = 0.044715
f32 = jnp.float32
bf16 = jnp.bfloat16
VMEM_LIMIT = 56 * 1024 * 1024
ANY = pl.BlockSpec(memory_space=pl.ANY)
LONG = 200_000_000_000


def swapped(array, axis, bit):
    return lax.ppermute(array, axis, [(i, i ^ 1 << bit) for i in range(lax.axis_size(axis))])


def after(value, *others):
    return lax.optimization_barrier((value,) + others)[0]


def cost(flops=1):
    return pl.CostEstimate(flops=flops, bytes_accessed=1, transcendentals=0)


def halo(array):
    peers = lax.axis_size("seq")
    up = [(i, i + 1) for i in range(peers - 1)]
    down = [(i + 1, i) for i in range(peers - 1)]
    rows = array.shape[0]
    before = lax.ppermute(lax.slice_in_dim(array, rows - 1, rows), "seq", up)
    behind = lax.ppermute(lax.slice_in_dim(array, 0, 1), "seq", down)
    return before, behind


def convolved_rows(x, before, behind, taps_ref, order):
    rows = x.shape[0]
    at = lax.broadcasted_iota(jnp.int32, x.shape, 0)
    earlier = jnp.where(at == 0, before.astype(f32), pltpu.roll(x, 1, 0))
    later = jnp.where(at == rows - 1, behind.astype(f32), pltpu.roll(x, rows - 1, 0))
    first, middle, last = order
    return (
        taps_ref[first : first + 1, :] * earlier
        + taps_ref[middle : middle + 1, :] * x
        + taps_ref[last : last + 1, :] * later
    ).astype(bf16)


def prepare_kernel(frames_ref, cot_ref, before_ref, behind_ref, taps_ref, grad_ref, *both_refs):
    grad = convolved_rows(cot_ref[...].astype(f32), before_ref[...], behind_ref[...], taps_ref, (2, 1, 0))
    grad_ref[...] = grad
    for j, both_ref in enumerate(both_refs):

        @pl.when(pl.program_id(0) == j + 1)
        def _():
            both_ref[0] = frames_ref[...]
            both_ref[1] = grad


def prepare(frames, cotangent, before, behind, taps, width):
    rows, local_width = frames.shape
    blocks = local_width // width
    column = lambda r: pl.BlockSpec((r, width), lambda i: (0, i))
    outs = pl.pallas_call(
        prepare_kernel,
        out_shape=[jax.ShapeDtypeStruct((rows, local_width), bf16)]
        + [jax.ShapeDtypeStruct((2, rows, width), bf16)] * (blocks - 1),
        grid=(blocks,),
        in_specs=[column(rows), column(rows), column(1), column(1), column(3)],
        out_specs=[column(rows)] + [pl.BlockSpec((2, rows, width), lambda i: (0, 0, 0))] * (blocks - 1),
        compiler_params=pltpu.CompilerParams(vmem_limit_bytes=VMEM_LIMIT),
        cost_estimate=cost(),
        name="prepare",
    )(frames, cotangent, before, behind, taps)
    return outs[0], outs[1:]


def convolution_kernel(x_ref, before_ref, behind_ref, taps_ref, out_ref, *, order):
    out_ref[...] = convolved_rows(x_ref[...].astype(f32), before_ref[...], behind_ref[...], taps_ref, order)


def convolution(x, before, behind, taps, order, width, blocks, flops=1):
    rows = x.shape[0]
    column = lambda r: pl.BlockSpec((r, width), lambda i: (0, i))
    return pl.pallas_call(
        functools.partial(convolution_kernel, order=order),
        out_shape=jax.ShapeDtypeStruct((rows, blocks * width), bf16),
        grid=(blocks,),
        in_specs=[column(rows), column(1), column(1), column(3)],
        out_specs=column(rows),
        compiler_params=pltpu.CompilerParams(vmem_limit_bytes=VMEM_LIMIT),
        cost_estimate=cost(flops),
        name="convolution",
    )(x, before, behind, taps)


def pair_parts(kept_ref, got_ref, bit):
    parts = [[], []]
    for r in range(kept_ref.shape[0]):
        total = (kept_ref[r].astype(f32) + got_ref[r].astype(f32)).astype(bf16)
        parts[r >> bit & 1].append(total)
    return parts


def level_index(level_bits, bit, levels):
    at = jnp.int32(0)
    for level in range(levels):
        at = at + jnp.where(level_bits[level] == bit, level + 1, 0)
    return at


def layer_kernel(level_bits, pattern, place, *refs, block, ratio, levels, peers, scale, older):
    terms = 1 + levels
    x_refs, refs = refs[:terms], refs[terms:]
    g_refs, refs = refs[:terms], refs[terms:]
    u_ref, d_ref = refs[:2]
    refs = refs[2:]
    if older:
        old_refs, refs = refs[:4], refs[4:]
    up_sent, up_kept, down_sent, down_kept, hidden_ref, grad_ref = refs[:6]
    refs = refs[6:]
    if older:
        (up_last, down_last), refs = refs[:2], refs[2:]
    x_all, x_turned, g_all, u_all, d_all, turned = refs
    h = pl.program_id(0)
    rows, width = x_refs[0].shape
    slab = width // peers
    k = block * ratio + h
    me = place[0]
    stages = peers.bit_length() - 1
    level_at = [level_index(level_bits, bit, levels) for bit in range(levels)]
    present = [pattern[k, at - 1] for at in level_at]

    @pl.when(h == 0)
    def _():
        for b in range(terms):
            value = x_refs[b][...]
            x_all[:, b * width : (b + 1) * width] = value
            g_all[:, b * width : (b + 1) * width] = g_refs[b][...]
            turned[...] = value.T
            for r in range(peers):
                start = pl.multiple_of((me ^ r) * slab, slab)
                x_turned[b * width + r * slab : b * width + (r + 1) * slab, :] = turned[pl.ds(start, slab), :]

    if older:
        up_parts = pair_parts(old_refs[0], old_refs[1], 0)
        down_parts = pair_parts(old_refs[2], old_refs[3], 0)
        up_last[0], down_sent[2] = up_parts[0][0], up_parts[1][0]
        down_last[0], up_sent[2] = down_parts[0][0], down_parts[1][0]

    for b in range(terms):
        if b == 0:
            u, d = u_ref[0, 0], d_ref[0, 0]
        else:
            mask = present[b - 1].astype(f32).astype(bf16)
            u, d = u_ref[level_at[b - 1], 0] * mask, d_ref[level_at[b - 1], 0] * mask
        u_all[b * width : (b + 1) * width, :] = u
        d_all[:, b * width : (b + 1) * width] = d

    pre = jnp.dot(x_all[...], u_all[...], preferred_element_type=f32)
    grad_hidden = lax.dot_general(
        g_all[...], d_all[...], (((1,), (1,)), ((), ())), preferred_element_type=f32
    )
    square = pre * pre
    inner = jnp.tanh(coef * (pre + cubic * (square * pre)))
    half = 0.5 * (1.0 + inner)
    slope = half + (0.5 * coef) * pre * (1.0 - inner * inner) * (1.0 + (3.0 * cubic) * square)
    hidden = (pre * half).astype(bf16)
    hidden_ref[...] = hidden
    turned[...] = hidden.T
    hidden_turned = jnp.concatenate(
        [
            turned[pl.ds(pl.multiple_of((me ^ r) * slab, slab), slab), :]
            for r in range(peers)
        ],
        axis=0,
    )
    grad_pre = (grad_hidden * slope).astype(bf16)
    grad_ref[...] = grad_pre

    for b in range(terms):
        span = slice(b * width, (b + 1) * width)
        up = jnp.dot(x_turned[span, :], grad_pre, preferred_element_type=f32)
        down = jnp.dot(hidden_turned, g_all[:, span], preferred_element_type=f32)
        if b == 0:
            factor, slot = scale, 0
        else:
            factor, slot = present[b - 1].astype(f32) * scale, level_at[b - 1]
        up, down = (up * factor).astype(bf16), (down * factor).astype(bf16)
        for value, sent, kept, bit in ((up, up_sent, up_kept, 0), (down, down_sent, down_kept, stages - 1)):
            counts = [0, 0]
            for r in range(peers):
                which = r >> bit & 1
                target = sent if which else kept
                target[counts[which], slot, 0] = value[r * slab : (r + 1) * slab, :]
                counts[which] += 1


def layer(level_bits, pattern, place, x, g, up_factors, down_factors, block, blocks_dev, peers, scale, older):
    terms, hidden_dev, width, _ = up_factors.shape
    levels = terms - 1
    rows = x[0][0].shape[0]
    ratio = hidden_dev // blocks_dev
    slab = width // peers
    inputs = [
        pl.BlockSpec((rows, width), lambda h, *s, at=at: at)
        if array.ndim == 2
        else pl.BlockSpec((None, rows, width), lambda h, *s, at=at: (at[0], 0, at[1]))
        for array, at in x + g
    ]
    weight = pl.BlockSpec((terms, 1, width, width), lambda h, *s: (0, block * ratio + h, 0, 0))
    piece = lambda n: pl.BlockSpec((n, terms, 1, slab, width), lambda h, *s: (0, 0, h, 0, 0))
    piece_shape = lambda n: jax.ShapeDtypeStruct((n, terms, ratio, slab, width), bf16)
    extra = [] if older is None else list(older)
    sums = [peers // 2 + (older is not None), peers // 2] * 2
    last = [] if older is None else [1, 1]
    outs = pl.pallas_call(
        functools.partial(
            layer_kernel,
            block=block,
            ratio=ratio,
            levels=levels,
            peers=peers,
            scale=scale,
            older=older is not None,
        ),
        out_shape=[piece_shape(n) for n in sums]
        + [jax.ShapeDtypeStruct((rows, ratio * width), bf16)] * 2
        + [piece_shape(n) for n in last],
        grid_spec=pltpu.PrefetchScalarGridSpec(
            num_scalar_prefetch=3,
            grid=(ratio,),
            in_specs=inputs + [weight] * 2 + [piece(2)] * len(extra),
            out_specs=[piece(n) for n in sums]
            + [pl.BlockSpec((rows, width), lambda h, *s: (0, h))] * 2
            + [piece(n) for n in last],
            scratch_shapes=[
                pltpu.VMEM((rows, terms * width), bf16),
                pltpu.VMEM((terms * width, rows), bf16),
                pltpu.VMEM((rows, terms * width), bf16),
                pltpu.VMEM((terms * width, width), bf16),
                pltpu.VMEM((width, terms * width), bf16),
                pltpu.VMEM((width, rows), bf16),
            ],
        ),
        compiler_params=pltpu.CompilerParams(vmem_limit_bytes=VMEM_LIMIT),
        cost_estimate=cost(LONG),
        name="layer",
    )(level_bits, pattern, place, *[array for array, _ in x + g], up_factors, down_factors, *extra)
    return outs[:4], outs[4], outs[5], outs[6:]


def terms_kernel(level_bits, pattern, hidden_ref, grad_ref, u_ref, d_ref, *refs, block, ratio, levels, local_bits, remote_bits):
    home_ref, *away_refs = refs[-1 - remote_bits :]
    b = pl.program_id(0)
    width = u_ref.shape[-1]
    at = level_index(level_bits, b - 1, levels)
    us, ds = [], []
    for h in range(ratio):
        present = jnp.where(b == 0, 1, pattern[block * ratio + h, jnp.maximum(at - 1, 0)])
        mask = present.astype(f32).astype(bf16)
        us.append(u_ref[0, h] * mask)
        ds.append(d_ref[0, h] * mask)
    mixed = jnp.dot(hidden_ref[...], jnp.concatenate(ds, axis=0), preferred_element_type=f32).astype(bf16)
    grad = lax.dot_general(
        grad_ref[...], jnp.concatenate(us, axis=1), (((1,), (1,)), ((), ())), preferred_element_type=f32
    ).astype(bf16)

    @pl.when(b <= local_bits)
    def _():
        home_ref[0, b], home_ref[1, b] = mixed, grad

    for bit, away_ref in enumerate(away_refs):

        @pl.when(b == 1 + local_bits + bit)
        def _():
            away_ref[0], away_ref[1] = mixed, grad


def term_sums(level_bits, pattern, hidden, grad, up_factors, down_factors, block, blocks_dev, together, away):
    terms, hidden_dev, width, _ = up_factors.shape
    levels = terms - 1
    rows = hidden.shape[0]
    ratio = hidden_dev // blocks_dev
    local_bits = blocks_dev.bit_length() - 1
    remote_bits = levels - local_bits
    whole = pl.BlockSpec((rows, ratio * width), lambda b, *s: (0, 0))
    weight = pl.BlockSpec(
        (1, ratio, width, width), lambda b, bits, *s: (level_index(bits, b - 1, levels), block, 0, 0)
    )
    extra = [] if away is None else list(away)
    outs = pl.pallas_call(
        functools.partial(
            terms_kernel, block=block, ratio=ratio, levels=levels, local_bits=local_bits, remote_bits=remote_bits
        ),
        out_shape=[jax.ShapeDtypeStruct((2, 1 + local_bits, rows, width), bf16)]
        + [jax.ShapeDtypeStruct((2 * together, rows, width), bf16)] * remote_bits,
        grid_spec=pltpu.PrefetchScalarGridSpec(
            num_scalar_prefetch=2,
            grid=(terms,),
            in_specs=[whole, whole, weight, weight] + [ANY] * len(extra),
            out_specs=[pl.BlockSpec((2, 1 + local_bits, rows, width), lambda b, *s: (0, 0, 0, 0))]
            + [pl.BlockSpec((2, rows, width), lambda b, *s: (block % together, 0, 0))] * remote_bits,
        ),
        input_output_aliases={6 + i: 1 + i for i in range(len(extra))},
        compiler_params=pltpu.CompilerParams(vmem_limit_bytes=VMEM_LIMIT),
        cost_estimate=cost(LONG if block == 0 else 1),
        name="term_sums",
    )(level_bits, pattern, hidden, grad, up_factors, down_factors, *extra)
    return outs[0], outs[1:]


def pair_kernel(*refs, bits):
    ins, outs = refs[: 2 * len(bits)], refs[2 * len(bits) :]
    for n, bit in enumerate(bits):
        kept, sent = pair_parts(ins[2 * n], ins[2 * n + 1], bit)
        for i, (a, b) in enumerate(zip(kept, sent)):
            outs[2 * n][i], outs[2 * n + 1][i] = a, b


def pair_sums(pairs, bits):
    parts, terms, blocks, slab, width = pairs[0][0].shape
    step = 2 if terms % 2 == 0 else 1
    spec = lambda n: pl.BlockSpec((n, terms // step, blocks, slab, width), lambda i: (0, i, 0, 0, 0))
    half = jax.ShapeDtypeStruct((parts // 2, terms, blocks, slab, width), bf16)
    outs = pl.pallas_call(
        functools.partial(pair_kernel, bits=bits),
        out_shape=[half] * 2 * len(pairs),
        grid=(step,),
        in_specs=[spec(parts)] * 2 * len(pairs),
        out_specs=[spec(parts // 2)] * 2 * len(pairs),
        compiler_params=pltpu.CompilerParams(vmem_limit_bytes=VMEM_LIMIT),
        cost_estimate=cost(LONG),
        name="pair_sums",
    )(*[array for pair in pairs for array in pair])
    return [outs[2 * i : 2 * i + 2] for i in range(len(pairs))]


def finish_kernel(a_kept, a_got, b_kept, b_got, *refs):
    a_out, b_out = refs[-2:]
    a_out[...] = a_kept[0].astype(f32) + a_got[0].astype(f32)
    b_out[...] = b_kept[0].astype(f32) + b_got[0].astype(f32)


def finish(a_kept, a_got, b_kept, b_got, outs, first, hidden_dev):
    _, terms, blocks, slab, width = a_kept.shape
    step = 2 if terms % 2 == 0 else 1
    spec = lambda array: pl.BlockSpec(
        (1, terms // step, blocks, slab, width), lambda i, row=array.shape[0] - 1: (row, i, 0, 0, 0)
    )
    out_spec = pl.BlockSpec((terms // step, blocks, slab, width), lambda i: (i, first // blocks, 0, 0))
    shape = jax.ShapeDtypeStruct((terms, hidden_dev, slab, width), f32)
    extra = [] if outs is None else list(outs)
    return pl.pallas_call(
        finish_kernel,
        out_shape=[shape, shape],
        grid=(step,),
        in_specs=[spec(array) for array in (a_kept, a_got, b_kept, b_got)] + [ANY] * len(extra),
        out_specs=[out_spec] * 2,
        input_output_aliases={4 + i: i for i in range(len(extra))},
        compiler_params=pltpu.CompilerParams(vmem_limit_bytes=VMEM_LIMIT),
        cost_estimate=cost(),
        name="finish",
    )(a_kept, a_got, b_kept, b_got, *extra)


def combine_kernel(*refs, blocks_dev, remote_bits, local_bits):
    homes, refs = refs[:blocks_dev], refs[blocks_dev:]
    aways, (mixed_ref, grad_ref) = refs[:-2], refs[-2:]
    width = homes[0].shape[-1]
    for j in range(blocks_dev):
        for side, target in ((0, mixed_ref), (1, grad_ref)):
            total = homes[j][side, 0].astype(f32)
            for bit in range(local_bits):
                total = total + homes[j ^ 1 << bit][side, 1 + bit].astype(f32)
            for bit in range(remote_bits):
                total = total + aways[j * remote_bits + bit][side].astype(f32)
            target[:, j * width : (j + 1) * width] = total.astype(bf16)


def combine(homes, aways, together):
    rows, width = homes[0].shape[-2:]
    blocks_dev = len(homes)
    local_bits, remote_bits = homes[0].shape[1] - 1, len(aways[0])
    chunk = min(rows, 128)
    home = pl.BlockSpec((2, 1 + local_bits, chunk, width), lambda i: (0, 0, i, 0))
    away = [
        pl.BlockSpec((2, chunk, width), lambda i, at=j % together: (at, i, 0))
        for j in range(blocks_dev)
        for _ in range(remote_bits)
    ]
    out = pl.BlockSpec((chunk, blocks_dev * width), lambda i: (i, 0))
    shape = jax.ShapeDtypeStruct((rows, blocks_dev * width), bf16)
    return pl.pallas_call(
        functools.partial(combine_kernel, remote_bits=remote_bits, local_bits=local_bits, blocks_dev=blocks_dev),
        out_shape=[shape, shape],
        grid=(rows // chunk,),
        in_specs=[home] * blocks_dev + away,
        out_specs=[out, out],
        compiler_params=pltpu.CompilerParams(vmem_limit_bytes=VMEM_LIMIT),
        cost_estimate=cost(),
        name="combine",
    )(*homes, *[part for j in range(blocks_dev) for part in aways[j // together]])


def local(frames, up_factors, down_factors, pattern, level_bits, taps, cotangent):
    rows, local_width = frames.shape
    terms, hidden_dev, width, _ = up_factors.shape
    blocks_dev = local_width // width
    ratio = hidden_dev // blocks_dev
    levels = terms - 1
    local_bits = blocks_dev.bit_length() - 1
    remote_bits = levels - local_bits
    far = list(range(1, remote_bits))
    together = min(2, blocks_dev)
    peers = lax.axis_size("seq")
    stages = peers.bit_length() - 1
    scale = 1.0 / math.sqrt(rows * peers)
    place = lax.axis_index("seq").astype(jnp.int32).reshape(1)

    def fetch(pieces, bits):
        got = {bit: swapped(pieces[bit], "tensor", bit) for bit in reversed(bits)}
        return [got[bit] for bit in bits]

    first = jnp.concatenate([frames[:, :width], frames[:16, :width]])
    x_first = fetch({bit: first for bit in far}, far)
    x_near = swapped(frames, "tensor", 0)
    before, behind = halo(cotangent)
    before = after(before, x_near)
    g_block = convolution(cotangent, before, behind, taps, (2, 1, 0), width, 1)
    g_first = fetch({bit: g_block for bit in far}, far)
    g_near_first = swapped(g_block, "tensor", 0)
    grad_mixed, both = prepare(frames, cotangent, after(before, g_block), behind, taps, width)
    g_near = swapped(grad_mixed, "tensor", 0)
    x_away = {0: [(value, (0, 0)) for value in x_first]}
    g_away = {0: [(value, (0, 0)) for value in g_first]}
    guards = [x_first, g_first]

    def fetch_far(pieces, *others):
        arrived = fetch({bit: after(pieces[bit], *[g[i] for g in guards], *others) for i, bit in enumerate(far)}, far)
        guards[:] = [arrived]
        return arrived

    def fetch_block(j, *others):
        arrived = fetch_far({bit: both[j - 1] for bit in far}, *others)
        x_away[j] = [(value, (0, 0)) for value in arrived]
        g_away[j] = [(value, (1, 0)) for value in arrived]

    if blocks_dev > 1:
        fetch_block(1)

    homes, aways, sums = [], [], {}
    merged = stages == 2
    x_got, y_got = {}, {}
    away = None
    made = []

    def give_terms(j, *others):
        nonlocal away
        hidden, grad_pre = made[j]
        home, away = term_sums(
            level_bits, pattern, after(hidden, *others) if others else hidden, grad_pre, up_factors, down_factors,
            j, blocks_dev, together, None if j % together == 0 else away,
        )
        homes.append(home)
        if (j + 1) % together == 0:
            aways.append((away[0], fetch_far(away)))

    for j in range(blocks_dev):
        older = None
        if merged and j >= 2:
            older = (sums[j - 2][0], x_got[j - 2], sums[j - 2][1], y_got[j - 2])
        flips = [0] + [1 << bit for bit in range(local_bits)]
        x = [(frames, (0, j ^ flip)) for flip in flips] + [(x_near, (0, j))] + x_away[j]
        g_near_block = (g_near_first, (0, 0)) if j == 0 else (g_near, (0, j))
        g = [(grad_mixed, (0, j ^ flip)) for flip in flips] + [g_near_block] + g_away[j]
        (up_sent, up_kept, down_sent, down_kept), hidden, grad_pre, last = layer(
            level_bits, pattern, place, x, g, up_factors, down_factors, j, blocks_dev, peers, scale, older
        )
        sums[j] = (up_kept, down_kept)
        if older is not None:
            sums[j - 2] = tuple(last)
        if j > 0:
            up_sent, down_sent = after(up_sent, x_got[j - 1]), after(down_sent, y_got[j - 1])
        x_got[j] = swapped(up_sent, "seq", 0)
        y_got[j] = swapped(down_sent, "seq", stages - 1)
        made.append((hidden, grad_pre))
        if j == 0:
            give_terms(0)
        if j + 2 < blocks_dev:
            fetch_block(j + 2, homes[0] if j == 0 else hidden)
        if j >= 2:
            give_terms(j - 1, hidden)
        if 0 < j == blocks_dev - 1:
            give_terms(j)

    def combined(*others):
        groups = []
        for near, rest in aways:
            groups.append([swapped(after(near, *others) if others else near, "tensor", 0)] + rest)
        mixed, grad_frames = combine(homes, groups, together)
        return mixed, grad_frames, *halo(mixed)

    outs = None
    if merged:

        def end(j):
            return (sums[j][0], y_got[j + 2], sums[j][1], x_got[j + 2])

        for j in range(max(blocks_dev - 2, 0), blocks_dev):
            got = [x_got[j], y_got[j]]
            if j == blocks_dev - 1:
                mixed, grad_frames, before, behind = combined(*([sums[j - 1][0]] if j else []))
                for done in range(blocks_dev - 3):
                    outs = finish(*end(done), outs, done * ratio, hidden_dev)
                got = [after(value, before, behind, *(outs or [])) for value in got]
            (up_last, up_next), (down_last, down_next) = pair_sums([(sums[j][0], got[0]), (sums[j][1], got[1])], (0, 0))
            if j + 1 < blocks_dev:
                down_next, up_next = after(down_next, x_got[j + 1]), after(up_next, y_got[j + 1])
            x_got[j + 2] = swapped(down_next, "seq", 0)
            y_got[j + 2] = swapped(up_next, "seq", 1)
            sums[j] = (up_last, down_last)
        convolved = convolution(mixed, before, behind, taps, (0, 1, 2), width, blocks_dev)
        for j in range(max(blocks_dev - 3, 0), blocks_dev):
            kept, got, down_kept, down_got = end(j)
            if j == blocks_dev - 2:
                got = after(got, convolved)
            outs = finish(kept, got, down_kept, down_got, outs, j * ratio, hidden_dev)
    else:
        for j in range(blocks_dev):
            got = [x_got[j], y_got[j]]
            kept = list(sums[j])
            orders = (list(range(stages)), list(range(stages))[::-1])
            for stage in range(1, stages):
                at = [sorted(order[stage:]).index(order[stage]) for order in orders]
                halves = pair_sums(list(zip(kept, got)), at)
                for side, order in enumerate(orders):
                    kept[side], sent = halves[side]
                    got[side] = swapped(sent, "seq", order[stage])
            outs = finish(kept[0], got[0], kept[1], got[1], outs, j * ratio, hidden_dev)
        mixed, grad_frames, before, behind = combined()
        convolved = convolution(mixed, before, behind, taps, (0, 1, 2), width, blocks_dev)
    return convolved, grad_frames, outs[0], outs[1]


def solution(mesh):
    in_specs = (
        P("seq", "tensor"),
        P(None, "tensor", None, None),
        P(None, "tensor", None, None),
        P("tensor", None),
        P(),
        P(None, "tensor"),
        P("seq", "tensor"),
    )
    out_specs = (
        P("seq", "tensor"),
        P("seq", "tensor"),
        P(None, "tensor", "seq", None),
        P(None, "tensor", "seq", None),
    )
    return jax.shard_map(local, mesh=mesh, in_specs=in_specs, out_specs=out_specs, check_vma=False)
```

```python
import functools
import math

import jax
import jax.numpy as jnp
from jax import lax
from jax.experimental import pallas as pl
from jax.experimental.pallas import tpu as pltpu
from jax.sharding import PartitionSpec as P

coef = 0.7978845608028654
cubic = 0.044715
f32 = jnp.float32
bf16 = jnp.bfloat16
VMEM_LIMIT = 56 * 1024 * 1024
ANY = pl.BlockSpec(memory_space=pl.ANY)
LONG = 200_000_000_000


def swapped(array, axis, bit):
    return lax.ppermute(array, axis, [(i, i ^ 1 << bit) for i in range(lax.axis_size(axis))])


def after(value, *others):
    return lax.optimization_barrier((value,) + others)[0]


def cost(flops=1):
    return pl.CostEstimate(flops=flops, bytes_accessed=1, transcendentals=0)


def halo(array):
    peers = lax.axis_size("seq")
    up = [(i, i + 1) for i in range(peers - 1)]
    down = [(i + 1, i) for i in range(peers - 1)]
    rows = array.shape[0]
    before = lax.ppermute(lax.slice_in_dim(array, rows - 1, rows), "seq", up)
    behind = lax.ppermute(lax.slice_in_dim(array, 0, 1), "seq", down)
    return before, behind


def convolved_rows(x, before, behind, taps_ref, order):
    rows = x.shape[0]
    at = lax.broadcasted_iota(jnp.int32, x.shape, 0)
    earlier = jnp.where(at == 0, before.astype(f32), pltpu.roll(x, 1, 0))
    later = jnp.where(at == rows - 1, behind.astype(f32), pltpu.roll(x, rows - 1, 0))
    first, middle, last = order
    return (
        taps_ref[first : first + 1, :] * earlier
        + taps_ref[middle : middle + 1, :] * x
        + taps_ref[last : last + 1, :] * later
    ).astype(bf16)


def prepare_kernel(frames_ref, cot_ref, before_ref, behind_ref, taps_ref, grad_ref, *both_refs):
    grad = convolved_rows(cot_ref[...].astype(f32), before_ref[...], behind_ref[...], taps_ref, (2, 1, 0))
    grad_ref[...] = grad
    for j, both_ref in enumerate(both_refs):

        @pl.when(pl.program_id(0) == j + 1)
        def _():
            both_ref[0] = frames_ref[...]
            both_ref[1] = grad


def prepare(frames, cotangent, before, behind, taps, width):
    rows, local_width = frames.shape
    blocks = local_width // width
    column = lambda r: pl.BlockSpec((r, width), lambda i: (0, i))
    outs = pl.pallas_call(
        prepare_kernel,
        out_shape=[jax.ShapeDtypeStruct((rows, local_width), bf16)]
        + [jax.ShapeDtypeStruct((2, rows, width), bf16)] * (blocks - 1),
        grid=(blocks,),
        in_specs=[column(rows), column(rows), column(1), column(1), column(3)],
        out_specs=[column(rows)] + [pl.BlockSpec((2, rows, width), lambda i: (0, 0, 0))] * (blocks - 1),
        compiler_params=pltpu.CompilerParams(vmem_limit_bytes=VMEM_LIMIT),
        cost_estimate=cost(),
        name="prepare",
    )(frames, cotangent, before, behind, taps)
    return outs[0], outs[1:]


def convolution_kernel(x_ref, before_ref, behind_ref, taps_ref, out_ref, *, order):
    out_ref[...] = convolved_rows(x_ref[...].astype(f32), before_ref[...], behind_ref[...], taps_ref, order)


def convolution(x, before, behind, taps, order, width, blocks, flops=1):
    rows = x.shape[0]
    column = lambda r: pl.BlockSpec((r, width), lambda i: (0, i))
    return pl.pallas_call(
        functools.partial(convolution_kernel, order=order),
        out_shape=jax.ShapeDtypeStruct((rows, blocks * width), bf16),
        grid=(blocks,),
        in_specs=[column(rows), column(1), column(1), column(3)],
        out_specs=column(rows),
        compiler_params=pltpu.CompilerParams(vmem_limit_bytes=VMEM_LIMIT),
        cost_estimate=cost(flops),
        name="convolution",
    )(x, before, behind, taps)


def pair_parts(kept_ref, got_ref, bit):
    parts = [[], []]
    for r in range(kept_ref.shape[0]):
        total = (kept_ref[r].astype(f32) + got_ref[r].astype(f32)).astype(bf16)
        parts[r >> bit & 1].append(total)
    return parts


def level_index(level_bits, bit, levels):
    at = jnp.int32(0)
    for level in range(levels):
        at = at + jnp.where(level_bits[level] == bit, level + 1, 0)
    return at


def layer_kernel(level_bits, pattern, place, *refs, block, ratio, levels, peers, scale, older):
    terms = 1 + levels
    x_refs, refs = refs[:terms], refs[terms:]
    g_refs, refs = refs[:terms], refs[terms:]
    u_ref, d_ref = refs[:2]
    refs = refs[2:]
    if older:
        old_refs, refs = refs[:4], refs[4:]
    up_sent, up_kept, down_sent, down_kept, hidden_ref, grad_ref = refs[:6]
    refs = refs[6:]
    if older:
        (up_last, down_last), refs = refs[:2], refs[2:]
    x_all, x_turned, g_all, u_all, d_all, turned = refs
    h = pl.program_id(0)
    rows, width = x_refs[0].shape
    slab = width // peers
    k = block * ratio + h
    me = place[0]
    stages = peers.bit_length() - 1
    level_at = [level_index(level_bits, bit, levels) for bit in range(levels)]
    present = [pattern[k, at - 1] for at in level_at]

    @pl.when(h == 0)
    def _():
        for b in range(terms):
            value = x_refs[b][...]
            x_all[:, b * width : (b + 1) * width] = value
            g_all[:, b * width : (b + 1) * width] = g_refs[b][...]
            turned[...] = value.T
            for r in range(peers):
                start = pl.multiple_of((me ^ r) * slab, slab)
                x_turned[b * width + r * slab : b * width + (r + 1) * slab, :] = turned[pl.ds(start, slab), :]

    if older:
        up_parts = pair_parts(old_refs[0], old_refs[1], 0)
        down_parts = pair_parts(old_refs[2], old_refs[3], 0)
        up_last[0], down_sent[2] = up_parts[0][0], up_parts[1][0]
        down_last[0], up_sent[2] = down_parts[0][0], down_parts[1][0]

    for b in range(terms):
        if b == 0:
            u, d = u_ref[0, 0], d_ref[0, 0]
        else:
            mask = present[b - 1].astype(f32).astype(bf16)
            u, d = u_ref[level_at[b - 1], 0] * mask, d_ref[level_at[b - 1], 0] * mask
        u_all[b * width : (b + 1) * width, :] = u
        d_all[:, b * width : (b + 1) * width] = d

    pre = jnp.dot(x_all[...], u_all[...], preferred_element_type=f32)
    grad_hidden = lax.dot_general(
        g_all[...], d_all[...], (((1,), (1,)), ((), ())), preferred_element_type=f32
    )
    square = pre * pre
    inner = jnp.tanh(coef * (pre + cubic * (square * pre)))
    half = 0.5 * (1.0 + inner)
    slope = half + (0.5 * coef) * pre * (1.0 - inner * inner) * (1.0 + (3.0 * cubic) * square)
    hidden = (pre * half).astype(bf16)
    hidden_ref[...] = hidden
    turned[...] = hidden.T
    hidden_turned = jnp.concatenate(
        [
            turned[pl.ds(pl.multiple_of((me ^ r) * slab, slab), slab), :]
            for r in range(peers)
        ],
        axis=0,
    )
    grad_pre = (grad_hidden * slope).astype(bf16)
    grad_ref[...] = grad_pre

    for b in range(terms):
        span = slice(b * width, (b + 1) * width)
        up = jnp.dot(x_turned[span, :], grad_pre, preferred_element_type=f32)
        down = jnp.dot(hidden_turned, g_all[:, span], preferred_element_type=f32)
        if b == 0:
            factor, slot = scale, 0
        else:
            factor, slot = present[b - 1].astype(f32) * scale, level_at[b - 1]
        up, down = (up * factor).astype(bf16), (down * factor).astype(bf16)
        for value, sent, kept, bit in ((up, up_sent, up_kept, 0), (down, down_sent, down_kept, stages - 1)):
            counts = [0, 0]
            for r in range(peers):
                which = r >> bit & 1
                target = sent if which else kept
                target[counts[which], slot, 0] = value[r * slab : (r + 1) * slab, :]
                counts[which] += 1


def layer(level_bits, pattern, place, x, g, up_factors, down_factors, block, blocks_dev, peers, scale, older):
    terms, hidden_dev, width, _ = up_factors.shape
    levels = terms - 1
    rows = x[0][0].shape[0]
    ratio = hidden_dev // blocks_dev
    slab = width // peers
    inputs = [
        pl.BlockSpec((rows, width), lambda h, *s, at=at: at)
        if array.ndim == 2
        else pl.BlockSpec((None, rows, width), lambda h, *s, at=at: (at[0], 0, at[1]))
        for array, at in x + g
    ]
    weight = pl.BlockSpec((terms, 1, width, width), lambda h, *s: (0, block * ratio + h, 0, 0))
    piece = lambda n: pl.BlockSpec((n, terms, 1, slab, width), lambda h, *s: (0, 0, h, 0, 0))
    piece_shape = lambda n: jax.ShapeDtypeStruct((n, terms, ratio, slab, width), bf16)
    extra = [] if older is None else list(older)
    sums = [peers // 2 + (older is not None), peers // 2] * 2
    last = [] if older is None else [1, 1]
    outs = pl.pallas_call(
        functools.partial(
            layer_kernel,
            block=block,
            ratio=ratio,
            levels=levels,
            peers=peers,
            scale=scale,
            older=older is not None,
        ),
        out_shape=[piece_shape(n) for n in sums]
        + [jax.ShapeDtypeStruct((rows, ratio * width), bf16)] * 2
        + [piece_shape(n) for n in last],
        grid_spec=pltpu.PrefetchScalarGridSpec(
            num_scalar_prefetch=3,
            grid=(ratio,),
            in_specs=inputs + [weight] * 2 + [piece(2)] * len(extra),
            out_specs=[piece(n) for n in sums]
            + [pl.BlockSpec((rows, width), lambda h, *s: (0, h))] * 2
            + [piece(n) for n in last],
            scratch_shapes=[
                pltpu.VMEM((rows, terms * width), bf16),
                pltpu.VMEM((terms * width, rows), bf16),
                pltpu.VMEM((rows, terms * width), bf16),
                pltpu.VMEM((terms * width, width), bf16),
                pltpu.VMEM((width, terms * width), bf16),
                pltpu.VMEM((width, rows), bf16),
            ],
        ),
        compiler_params=pltpu.CompilerParams(vmem_limit_bytes=VMEM_LIMIT),
        cost_estimate=cost(LONG),
        name="layer",
    )(level_bits, pattern, place, *[array for array, _ in x + g], up_factors, down_factors, *extra)
    return outs[:4], outs[4], outs[5], outs[6:]


def terms_kernel(level_bits, pattern, hidden_ref, grad_ref, u_ref, d_ref, *refs, block, ratio, levels, local_bits, remote_bits):
    home_ref, *away_refs = refs[-1 - remote_bits :]
    b = pl.program_id(0)
    width = u_ref.shape[-1]
    at = level_index(level_bits, b - 1, levels)
    us, ds = [], []
    for h in range(ratio):
        present = jnp.where(b == 0, 1, pattern[block * ratio + h, jnp.maximum(at - 1, 0)])
        mask = present.astype(f32).astype(bf16)
        us.append(u_ref[0, h] * mask)
        ds.append(d_ref[0, h] * mask)
    mixed = jnp.dot(hidden_ref[...], jnp.concatenate(ds, axis=0), preferred_element_type=f32).astype(bf16)
    grad = lax.dot_general(
        grad_ref[...], jnp.concatenate(us, axis=1), (((1,), (1,)), ((), ())), preferred_element_type=f32
    ).astype(bf16)

    @pl.when(b <= local_bits)
    def _():
        home_ref[0, b], home_ref[1, b] = mixed, grad

    for bit, away_ref in enumerate(away_refs):

        @pl.when(b == 1 + local_bits + bit)
        def _():
            away_ref[0], away_ref[1] = mixed, grad


def term_sums(level_bits, pattern, hidden, grad, up_factors, down_factors, block, blocks_dev, together, away):
    terms, hidden_dev, width, _ = up_factors.shape
    levels = terms - 1
    rows = hidden.shape[0]
    ratio = hidden_dev // blocks_dev
    local_bits = blocks_dev.bit_length() - 1
    remote_bits = levels - local_bits
    whole = pl.BlockSpec((rows, ratio * width), lambda b, *s: (0, 0))
    weight = pl.BlockSpec(
        (1, ratio, width, width), lambda b, bits, *s: (level_index(bits, b - 1, levels), block, 0, 0)
    )
    extra = [] if away is None else list(away)
    outs = pl.pallas_call(
        functools.partial(
            terms_kernel, block=block, ratio=ratio, levels=levels, local_bits=local_bits, remote_bits=remote_bits
        ),
        out_shape=[jax.ShapeDtypeStruct((2, 1 + local_bits, rows, width), bf16)]
        + [jax.ShapeDtypeStruct((2 * together, rows, width), bf16)] * remote_bits,
        grid_spec=pltpu.PrefetchScalarGridSpec(
            num_scalar_prefetch=2,
            grid=(terms,),
            in_specs=[whole, whole, weight, weight] + [ANY] * len(extra),
            out_specs=[pl.BlockSpec((2, 1 + local_bits, rows, width), lambda b, *s: (0, 0, 0, 0))]
            + [pl.BlockSpec((2, rows, width), lambda b, *s: (block % together, 0, 0))] * remote_bits,
        ),
        input_output_aliases={6 + i: 1 + i for i in range(len(extra))},
        compiler_params=pltpu.CompilerParams(vmem_limit_bytes=VMEM_LIMIT),
        cost_estimate=cost(),
        name="term_sums",
    )(level_bits, pattern, hidden, grad, up_factors, down_factors, *extra)
    return outs[0], outs[1:]


def pair_kernel(*refs, bits):
    ins, outs = refs[: 2 * len(bits)], refs[2 * len(bits) :]
    for n, bit in enumerate(bits):
        kept, sent = pair_parts(ins[2 * n], ins[2 * n + 1], bit)
        for i, (a, b) in enumerate(zip(kept, sent)):
            outs[2 * n][i], outs[2 * n + 1][i] = a, b


def pair_sums(pairs, bits):
    parts, terms, blocks, slab, width = pairs[0][0].shape
    step = 2 if terms % 2 == 0 else 1
    spec = lambda n: pl.BlockSpec((n, terms // step, blocks, slab, width), lambda i: (0, i, 0, 0, 0))
    half = jax.ShapeDtypeStruct((parts // 2, terms, blocks, slab, width), bf16)
    outs = pl.pallas_call(
        functools.partial(pair_kernel, bits=bits),
        out_shape=[half] * 2 * len(pairs),
        grid=(step,),
        in_specs=[spec(parts)] * 2 * len(pairs),
        out_specs=[spec(parts // 2)] * 2 * len(pairs),
        compiler_params=pltpu.CompilerParams(vmem_limit_bytes=VMEM_LIMIT),
        cost_estimate=cost(LONG),
        name="pair_sums",
    )(*[array for pair in pairs for array in pair])
    return [outs[2 * i : 2 * i + 2] for i in range(len(pairs))]


def finish_kernel(a_kept, a_got, b_kept, b_got, *refs):
    a_out, b_out = refs[-2:]
    a_out[...] = a_kept[0].astype(f32) + a_got[0].astype(f32)
    b_out[...] = b_kept[0].astype(f32) + b_got[0].astype(f32)


def finish(a_kept, a_got, b_kept, b_got, outs, first, hidden_dev):
    _, terms, blocks, slab, width = a_kept.shape
    step = 2 if terms % 2 == 0 else 1
    spec = lambda array: pl.BlockSpec(
        (1, terms // step, blocks, slab, width), lambda i, row=array.shape[0] - 1: (row, i, 0, 0, 0)
    )
    out_spec = pl.BlockSpec((terms // step, blocks, slab, width), lambda i: (i, first // blocks, 0, 0))
    shape = jax.ShapeDtypeStruct((terms, hidden_dev, slab, width), f32)
    extra = [] if outs is None else list(outs)
    return pl.pallas_call(
        finish_kernel,
        out_shape=[shape, shape],
        grid=(step,),
        in_specs=[spec(array) for array in (a_kept, a_got, b_kept, b_got)] + [ANY] * len(extra),
        out_specs=[out_spec] * 2,
        input_output_aliases={4 + i: i for i in range(len(extra))},
        compiler_params=pltpu.CompilerParams(vmem_limit_bytes=VMEM_LIMIT),
        cost_estimate=cost(),
        name="finish",
    )(a_kept, a_got, b_kept, b_got, *extra)


def pause_kernel(_, out_ref):
    out_ref[...] = jnp.zeros(out_ref.shape, f32)


def pause(behind):
    return pl.pallas_call(
        pause_kernel,
        out_shape=jax.ShapeDtypeStruct((8, 128), f32),
        in_specs=[ANY],
        cost_estimate=cost(LONG),
        name="pause",
    )(behind)


def combine_kernel(*refs, blocks_dev, remote_bits, local_bits):
    homes, refs = refs[:blocks_dev], refs[blocks_dev:]
    aways, (mixed_ref, grad_ref) = refs[:-2], refs[-2:]
    width = homes[0].shape[-1]
    for j in range(blocks_dev):
        for side, target in ((0, mixed_ref), (1, grad_ref)):
            total = homes[j][side, 0].astype(f32)
            for bit in range(local_bits):
                total = total + homes[j ^ 1 << bit][side, 1 + bit].astype(f32)
            for bit in range(remote_bits):
                total = total + aways[j * remote_bits + bit][side].astype(f32)
            target[:, j * width : (j + 1) * width] = total.astype(bf16)


def combine(homes, aways, together):
    rows, width = homes[0].shape[-2:]
    blocks_dev = len(homes)
    local_bits, remote_bits = homes[0].shape[1] - 1, len(aways[0])
    chunk = min(rows, 128)
    home = pl.BlockSpec((2, 1 + local_bits, chunk, width), lambda i: (0, 0, i, 0))
    away = [
        pl.BlockSpec((2, chunk, width), lambda i, at=j % together: (at, i, 0))
        for j in range(blocks_dev)
        for _ in range(remote_bits)
    ]
    out = pl.BlockSpec((chunk, blocks_dev * width), lambda i: (i, 0))
    shape = jax.ShapeDtypeStruct((rows, blocks_dev * width), bf16)
    return pl.pallas_call(
        functools.partial(combine_kernel, remote_bits=remote_bits, local_bits=local_bits, blocks_dev=blocks_dev),
        out_shape=[shape, shape],
        grid=(rows // chunk,),
        in_specs=[home] * blocks_dev + away,
        out_specs=[out, out],
        compiler_params=pltpu.CompilerParams(vmem_limit_bytes=VMEM_LIMIT),
        cost_estimate=cost(),
        name="combine",
    )(*homes, *[part for j in range(blocks_dev) for part in aways[j // together]])


def local(frames, up_factors, down_factors, pattern, level_bits, taps, cotangent):
    rows, local_width = frames.shape
    terms, hidden_dev, width, _ = up_factors.shape
    blocks_dev = local_width // width
    ratio = hidden_dev // blocks_dev
    levels = terms - 1
    local_bits = blocks_dev.bit_length() - 1
    remote_bits = levels - local_bits
    far = list(range(1, remote_bits))
    together = min(2, blocks_dev)
    peers = lax.axis_size("seq")
    stages = peers.bit_length() - 1
    scale = 1.0 / math.sqrt(rows * peers)
    place = lax.axis_index("seq").astype(jnp.int32).reshape(1)

    def fetch(pieces, bits):
        got = {bit: swapped(pieces[bit], "tensor", bit) for bit in reversed(bits)}
        return [got[bit] for bit in bits]

    first = lax.pad(frames[:, :width], jnp.zeros((), frames.dtype), ((0, 16, 0), (0, 0, 0)))
    x_first = fetch({bit: first for bit in far}, far)
    x_near = swapped(frames, "tensor", 0)
    before, behind = halo(cotangent)
    before = after(before, x_near)
    g_block = convolution(cotangent, before, behind, taps, (2, 1, 0), width, 1)
    g_first = fetch({bit: g_block for bit in far}, far)
    g_near_first = swapped(g_block, "tensor", 0)
    grad_mixed, both = prepare(frames, cotangent, after(before, g_block), behind, taps, width)
    g_near = swapped(grad_mixed, "tensor", 0)
    x_away = {0: [(value, (0, 0)) for value in x_first]}
    g_away = {0: [(value, (0, 0)) for value in g_first]}
    guards = [x_first, g_first]

    def fetch_far(pieces, *others):
        arrived = fetch({bit: after(pieces[bit], *[g[i] for g in guards], *others) for i, bit in enumerate(far)}, far)
        guards[:] = [arrived]
        return arrived

    def fetch_block(j, *others):
        arrived = fetch_far({bit: both[j - 1] for bit in far}, *others)
        x_away[j] = [(value, (0, 0)) for value in arrived]
        g_away[j] = [(value, (1, 0)) for value in arrived]

    if blocks_dev > 1:
        fetch_block(1)

    homes, aways, sums = [], [], {}
    merged = stages == 2
    x_got, y_got = {}, {}
    away = None
    made = []

    def give_terms(j, *others):
        nonlocal away
        hidden, grad_pre = made[j]
        home, away = term_sums(
            level_bits, pattern, after(hidden, *others) if others else hidden, grad_pre, up_factors, down_factors,
            j, blocks_dev, together, None if j % together == 0 else away,
        )
        homes.append(home)
        if (j + 1) % together == 0:
            aways.append((away[0], fetch_far(away)))

    for j in range(blocks_dev):
        older = None
        if merged and j >= 2:
            older = (sums[j - 2][0], x_got[j - 2], sums[j - 2][1], y_got[j - 2])
        flips = [0] + [1 << bit for bit in range(local_bits)]
        x = [(frames, (0, j ^ flip)) for flip in flips] + [(x_near, (0, j))] + x_away[j]
        g_near_block = (g_near_first, (0, 0)) if j == 0 else (g_near, (0, j))
        g = [(grad_mixed, (0, j ^ flip)) for flip in flips] + [g_near_block] + g_away[j]
        (up_sent, up_kept, down_sent, down_kept), hidden, grad_pre, last = layer(
            level_bits, pattern, place, x, g, up_factors, down_factors, j, blocks_dev, peers, scale, older
        )
        sums[j] = (up_kept, down_kept)
        if older is not None:
            sums[j - 2] = tuple(last)
        if j > 0:
            up_sent, down_sent = after(up_sent, x_got[j - 1]), after(down_sent, y_got[j - 1])
        x_got[j] = swapped(up_sent, "seq", 0)
        y_got[j] = swapped(down_sent, "seq", stages - 1)
        made.append((hidden, grad_pre))
        if j + 2 < blocks_dev:
            fetch_block(j + 2, pause(hidden) if j == 0 else hidden)
        if j >= 1:
            give_terms(j - 1, hidden)
        if j == blocks_dev - 1:
            give_terms(j)

    def combined(*others):
        groups = []
        for near, rest in aways:
            groups.append([swapped(after(near, *others) if others else near, "tensor", 0)] + rest)
        mixed, grad_frames = combine(homes, groups, together)
        return mixed, grad_frames, *halo(mixed)

    outs = None
    if merged:

        def end(j):
            return (sums[j][0], y_got[j + 2], sums[j][1], x_got[j + 2])

        for j in range(max(blocks_dev - 2, 0), blocks_dev):
            got = [x_got[j], y_got[j]]
            if j == blocks_dev - 1:
                for done in range(blocks_dev - 3):
                    outs = finish(*end(done), outs, done * ratio, hidden_dev)
                homes[0] = after(homes[0], *(outs or []))
                mixed, grad_frames, before, behind = combined(*([sums[j - 1][0]] if j else []))
                got = [after(value, before, behind) for value in got]
            (up_last, up_next), (down_last, down_next) = pair_sums([(sums[j][0], got[0]), (sums[j][1], got[1])], (0, 0))
            if j + 1 < blocks_dev:
                down_next, up_next = after(down_next, x_got[j + 1]), after(up_next, y_got[j + 1])
            x_got[j + 2] = swapped(down_next, "seq", 0)
            y_got[j + 2] = swapped(up_next, "seq", 1)
            sums[j] = (up_last, down_last)
        convolved = convolution(mixed, before, behind, taps, (0, 1, 2), width, blocks_dev)
        for j in range(max(blocks_dev - 3, 0), blocks_dev):
            kept, got, down_kept, down_got = end(j)
            if j == blocks_dev - 2:
                got = after(got, convolved)
            outs = finish(kept, got, down_kept, down_got, outs, j * ratio, hidden_dev)
    else:
        for j in range(blocks_dev):
            got = [x_got[j], y_got[j]]
            kept = list(sums[j])
            orders = (list(range(stages)), list(range(stages))[::-1])
            for stage in range(1, stages):
                at = [sorted(order[stage:]).index(order[stage]) for order in orders]
                halves = pair_sums(list(zip(kept, got)), at)
                for side, order in enumerate(orders):
                    kept[side], sent = halves[side]
                    got[side] = swapped(sent, "seq", order[stage])
            outs = finish(kept[0], got[0], kept[1], got[1], outs, j * ratio, hidden_dev)
        mixed, grad_frames, before, behind = combined()
        convolved = convolution(mixed, before, behind, taps, (0, 1, 2), width, blocks_dev)
    return convolved, grad_frames, outs[0], outs[1]


def solution(mesh):
    in_specs = (
        P("seq", "tensor"),
        P(None, "tensor", None, None),
        P(None, "tensor", None, None),
        P("tensor", None),
        P(),
        P(None, "tensor"),
        P("seq", "tensor"),
    )
    out_specs = (
        P("seq", "tensor"),
        P("seq", "tensor"),
        P(None, "tensor", "seq", None),
        P(None, "tensor", "seq", None),
    )
    return jax.shard_map(local, mesh=mesh, in_specs=in_specs, out_specs=out_specs, check_vma=False)
```

```python
import functools
import math

import jax
import jax.numpy as jnp
from jax import lax
from jax.experimental import pallas as pl
from jax.experimental.pallas import tpu as pltpu
from jax.sharding import PartitionSpec as P

coef = 0.7978845608028654
cubic = 0.044715
f32 = jnp.float32
bf16 = jnp.bfloat16
VMEM_LIMIT = 56 * 1024 * 1024
ANY = pl.BlockSpec(memory_space=pl.ANY)
LONG = 200_000_000_000


def swapped(array, axis, bit):
    return lax.ppermute(array, axis, [(i, i ^ 1 << bit) for i in range(lax.axis_size(axis))])


def after(value, *others):
    return lax.optimization_barrier((value,) + others)[0]


def cost(flops=1):
    return pl.CostEstimate(flops=flops, bytes_accessed=1, transcendentals=0)


def halo(array):
    peers = lax.axis_size("seq")
    up = [(i, i + 1) for i in range(peers - 1)]
    down = [(i + 1, i) for i in range(peers - 1)]
    rows = array.shape[0]
    before = lax.ppermute(lax.slice_in_dim(array, rows - 1, rows), "seq", up)
    behind = lax.ppermute(lax.slice_in_dim(array, 0, 1), "seq", down)
    return before, behind


def convolved_rows(x, before, behind, taps_ref, order):
    rows = x.shape[0]
    at = lax.broadcasted_iota(jnp.int32, x.shape, 0)
    earlier = jnp.where(at == 0, before.astype(f32), pltpu.roll(x, 1, 0))
    later = jnp.where(at == rows - 1, behind.astype(f32), pltpu.roll(x, rows - 1, 0))
    first, middle, last = order
    return (
        taps_ref[first : first + 1, :] * earlier
        + taps_ref[middle : middle + 1, :] * x
        + taps_ref[last : last + 1, :] * later
    ).astype(bf16)


def prepare_kernel(frames_ref, cot_ref, before_ref, behind_ref, taps_ref, grad_ref, *both_refs):
    grad = convolved_rows(cot_ref[...].astype(f32), before_ref[...], behind_ref[...], taps_ref, (2, 1, 0))
    grad_ref[...] = grad
    for j, both_ref in enumerate(both_refs):

        @pl.when(pl.program_id(0) == j + 1)
        def _():
            both_ref[0] = frames_ref[...]
            both_ref[1] = grad


def prepare(frames, cotangent, before, behind, taps, width):
    rows, local_width = frames.shape
    blocks = local_width // width
    column = lambda r: pl.BlockSpec((r, width), lambda i: (0, i))
    outs = pl.pallas_call(
        prepare_kernel,
        out_shape=[jax.ShapeDtypeStruct((rows, local_width), bf16)]
        + [jax.ShapeDtypeStruct((2, rows, width), bf16)] * (blocks - 1),
        grid=(blocks,),
        in_specs=[column(rows), column(rows), column(1), column(1), column(3)],
        out_specs=[column(rows)] + [pl.BlockSpec((2, rows, width), lambda i: (0, 0, 0))] * (blocks - 1),
        compiler_params=pltpu.CompilerParams(vmem_limit_bytes=VMEM_LIMIT),
        cost_estimate=cost(),
        name="prepare",
    )(frames, cotangent, before, behind, taps)
    return outs[0], outs[1:]


def convolution_kernel(x_ref, before_ref, behind_ref, taps_ref, out_ref, *, order):
    out_ref[...] = convolved_rows(x_ref[...].astype(f32), before_ref[...], behind_ref[...], taps_ref, order)


def convolution(x, before, behind, taps, order, width, blocks, flops=1):
    rows = x.shape[0]
    column = lambda r: pl.BlockSpec((r, width), lambda i: (0, i))
    return pl.pallas_call(
        functools.partial(convolution_kernel, order=order),
        out_shape=jax.ShapeDtypeStruct((rows, blocks * width), bf16),
        grid=(blocks,),
        in_specs=[column(rows), column(1), column(1), column(3)],
        out_specs=column(rows),
        compiler_params=pltpu.CompilerParams(vmem_limit_bytes=VMEM_LIMIT),
        cost_estimate=cost(flops),
        name="convolution",
    )(x, before, behind, taps)


def pair_parts(kept_ref, got_ref, bit):
    parts = [[], []]
    for r in range(kept_ref.shape[0]):
        total = (kept_ref[r].astype(f32) + got_ref[r].astype(f32)).astype(bf16)
        parts[r >> bit & 1].append(total)
    return parts


def level_index(level_bits, bit, levels):
    at = jnp.int32(0)
    for level in range(levels):
        at = at + jnp.where(level_bits[level] == bit, level + 1, 0)
    return at


def layer_kernel(level_bits, pattern, place, *refs, block, ratio, levels, peers, scale, older):
    terms = 1 + levels
    x_refs, refs = refs[:terms], refs[terms:]
    g_refs, refs = refs[:terms], refs[terms:]
    u_ref, d_ref = refs[:2]
    refs = refs[2:]
    if older:
        old_refs, refs = refs[:4], refs[4:]
    up_sent, up_kept, down_sent, down_kept, hidden_ref, grad_ref = refs[:6]
    refs = refs[6:]
    if older:
        (up_last, down_last), refs = refs[:2], refs[2:]
    x_all, x_turned, g_all, u_all, d_all, turned = refs
    h = pl.program_id(0)
    rows, width = x_refs[0].shape
    slab = width // peers
    k = block * ratio + h
    me = place[0]
    stages = peers.bit_length() - 1
    level_at = [level_index(level_bits, bit, levels) for bit in range(levels)]
    present = [pattern[k, at - 1] for at in level_at]

    @pl.when(h == 0)
    def _():
        for b in range(terms):
            value = x_refs[b][...]
            x_all[:, b * width : (b + 1) * width] = value
            g_all[:, b * width : (b + 1) * width] = g_refs[b][...]
            turned[...] = value.T
            for r in range(peers):
                start = pl.multiple_of((me ^ r) * slab, slab)
                x_turned[b * width + r * slab : b * width + (r + 1) * slab, :] = turned[pl.ds(start, slab), :]

    if older:
        up_parts = pair_parts(old_refs[0], old_refs[1], 0)
        down_parts = pair_parts(old_refs[2], old_refs[3], 0)
        up_last[0], down_sent[2] = up_parts[0][0], up_parts[1][0]
        down_last[0], up_sent[2] = down_parts[0][0], down_parts[1][0]

    for b in range(terms):
        if b == 0:
            u, d = u_ref[0, 0], d_ref[0, 0]
        else:
            mask = present[b - 1].astype(f32).astype(bf16)
            u, d = u_ref[level_at[b - 1], 0] * mask, d_ref[level_at[b - 1], 0] * mask
        u_all[b * width : (b + 1) * width, :] = u
        d_all[:, b * width : (b + 1) * width] = d

    pre = jnp.dot(x_all[...], u_all[...], preferred_element_type=f32)
    grad_hidden = lax.dot_general(
        g_all[...], d_all[...], (((1,), (1,)), ((), ())), preferred_element_type=f32
    )
    square = pre * pre
    inner = jnp.tanh(coef * (pre + cubic * (square * pre)))
    half = 0.5 * (1.0 + inner)
    slope = half + (0.5 * coef) * pre * (1.0 - inner * inner) * (1.0 + (3.0 * cubic) * square)
    hidden = (pre * half).astype(bf16)
    hidden_ref[...] = hidden
    turned[...] = hidden.T
    hidden_turned = jnp.concatenate(
        [
            turned[pl.ds(pl.multiple_of((me ^ r) * slab, slab), slab), :]
            for r in range(peers)
        ],
        axis=0,
    )
    grad_pre = (grad_hidden * slope).astype(bf16)
    grad_ref[...] = grad_pre

    for b in range(terms):
        span = slice(b * width, (b + 1) * width)
        up = jnp.dot(x_turned[span, :], grad_pre, preferred_element_type=f32)
        down = jnp.dot(hidden_turned, g_all[:, span], preferred_element_type=f32)
        if b == 0:
            factor, slot = scale, 0
        else:
            factor, slot = present[b - 1].astype(f32) * scale, level_at[b - 1]
        up, down = (up * factor).astype(bf16), (down * factor).astype(bf16)
        for value, sent, kept, bit in ((up, up_sent, up_kept, 0), (down, down_sent, down_kept, stages - 1)):
            counts = [0, 0]
            for r in range(peers):
                which = r >> bit & 1
                target = sent if which else kept
                target[counts[which], slot, 0] = value[r * slab : (r + 1) * slab, :]
                counts[which] += 1


def layer(level_bits, pattern, place, x, g, up_factors, down_factors, block, blocks_dev, peers, scale, older):
    terms, hidden_dev, width, _ = up_factors.shape
    levels = terms - 1
    rows = x[0][0].shape[0]
    ratio = hidden_dev // blocks_dev
    slab = width // peers
    inputs = [
        pl.BlockSpec((rows, width), lambda h, *s, at=at: at)
        if array.ndim == 2
        else pl.BlockSpec((None, rows, width), lambda h, *s, at=at: (at[0], 0, at[1]))
        for array, at in x + g
    ]
    weight = pl.BlockSpec((terms, 1, width, width), lambda h, *s: (0, block * ratio + h, 0, 0))
    piece = lambda n: pl.BlockSpec((n, terms, 1, slab, width), lambda h, *s: (0, 0, h, 0, 0))
    piece_shape = lambda n: jax.ShapeDtypeStruct((n, terms, ratio, slab, width), bf16)
    extra = [] if older is None else list(older)
    sums = [peers // 2 + (older is not None), peers // 2] * 2
    last = [] if older is None else [1, 1]
    outs = pl.pallas_call(
        functools.partial(
            layer_kernel,
            block=block,
            ratio=ratio,
            levels=levels,
            peers=peers,
            scale=scale,
            older=older is not None,
        ),
        out_shape=[piece_shape(n) for n in sums]
        + [jax.ShapeDtypeStruct((rows, ratio * width), bf16)] * 2
        + [piece_shape(n) for n in last],
        grid_spec=pltpu.PrefetchScalarGridSpec(
            num_scalar_prefetch=3,
            grid=(ratio,),
            in_specs=inputs + [weight] * 2 + [piece(2)] * len(extra),
            out_specs=[piece(n) for n in sums]
            + [pl.BlockSpec((rows, width), lambda h, *s: (0, h))] * 2
            + [piece(n) for n in last],
            scratch_shapes=[
                pltpu.VMEM((rows, terms * width), bf16),
                pltpu.VMEM((terms * width, rows), bf16),
                pltpu.VMEM((rows, terms * width), bf16),
                pltpu.VMEM((terms * width, width), bf16),
                pltpu.VMEM((width, terms * width), bf16),
                pltpu.VMEM((width, rows), bf16),
            ],
        ),
        compiler_params=pltpu.CompilerParams(vmem_limit_bytes=VMEM_LIMIT),
        cost_estimate=cost(LONG),
        name="layer",
    )(level_bits, pattern, place, *[array for array, _ in x + g], up_factors, down_factors, *extra)
    return outs[:4], outs[4], outs[5], outs[6:]


def terms_kernel(level_bits, pattern, hidden_ref, grad_ref, u_ref, d_ref, *refs, block, ratio, levels, local_bits, remote_bits):
    home_ref, *away_refs = refs[-1 - remote_bits :]
    b = pl.program_id(0)
    width = u_ref.shape[-1]
    at = level_index(level_bits, b - 1, levels)
    us, ds = [], []
    for h in range(ratio):
        present = jnp.where(b == 0, 1, pattern[block * ratio + h, jnp.maximum(at - 1, 0)])
        mask = present.astype(f32).astype(bf16)
        us.append(u_ref[0, h] * mask)
        ds.append(d_ref[0, h] * mask)
    mixed = jnp.dot(hidden_ref[...], jnp.concatenate(ds, axis=0), preferred_element_type=f32).astype(bf16)
    grad = lax.dot_general(
        grad_ref[...], jnp.concatenate(us, axis=1), (((1,), (1,)), ((), ())), preferred_element_type=f32
    ).astype(bf16)

    @pl.when(b <= local_bits)
    def _():
        home_ref[0, b], home_ref[1, b] = mixed, grad

    for bit, away_ref in enumerate(away_refs):

        @pl.when(b == 1 + local_bits + bit)
        def _():
            away_ref[0], away_ref[1] = mixed, grad


def term_sums(level_bits, pattern, hidden, grad, up_factors, down_factors, block, blocks_dev, together, away):
    terms, hidden_dev, width, _ = up_factors.shape
    levels = terms - 1
    rows = hidden.shape[0]
    ratio = hidden_dev // blocks_dev
    local_bits = blocks_dev.bit_length() - 1
    remote_bits = levels - local_bits
    whole = pl.BlockSpec((rows, ratio * width), lambda b, *s: (0, 0))
    weight = pl.BlockSpec(
        (1, ratio, width, width), lambda b, bits, *s: (level_index(bits, b - 1, levels), block, 0, 0)
    )
    extra = [] if away is None else list(away)
    outs = pl.pallas_call(
        functools.partial(
            terms_kernel, block=block, ratio=ratio, levels=levels, local_bits=local_bits, remote_bits=remote_bits
        ),
        out_shape=[jax.ShapeDtypeStruct((2, 1 + local_bits, rows, width), bf16)]
        + [jax.ShapeDtypeStruct((2 * together, rows, width), bf16)] * remote_bits,
        grid_spec=pltpu.PrefetchScalarGridSpec(
            num_scalar_prefetch=2,
            grid=(terms,),
            in_specs=[whole, whole, weight, weight] + [ANY] * len(extra),
            out_specs=[pl.BlockSpec((2, 1 + local_bits, rows, width), lambda b, *s: (0, 0, 0, 0))]
            + [pl.BlockSpec((2, rows, width), lambda b, *s: (block % together, 0, 0))] * remote_bits,
        ),
        input_output_aliases={6 + i: 1 + i for i in range(len(extra))},
        compiler_params=pltpu.CompilerParams(vmem_limit_bytes=VMEM_LIMIT),
        cost_estimate=cost(),
        name="term_sums",
    )(level_bits, pattern, hidden, grad, up_factors, down_factors, *extra)
    return outs[0], outs[1:]


def pair_kernel(*refs, bits):
    ins, outs = refs[: 2 * len(bits)], refs[2 * len(bits) :]
    for n, bit in enumerate(bits):
        kept, sent = pair_parts(ins[2 * n], ins[2 * n + 1], bit)
        for i, (a, b) in enumerate(zip(kept, sent)):
            outs[2 * n][i], outs[2 * n + 1][i] = a, b


def pair_sums(pairs, bits):
    parts, terms, blocks, slab, width = pairs[0][0].shape
    step = 2 if terms % 2 == 0 else 1
    spec = lambda n: pl.BlockSpec((n, terms // step, blocks, slab, width), lambda i: (0, i, 0, 0, 0))
    half = jax.ShapeDtypeStruct((parts // 2, terms, blocks, slab, width), bf16)
    outs = pl.pallas_call(
        functools.partial(pair_kernel, bits=bits),
        out_shape=[half] * 2 * len(pairs),
        grid=(step,),
        in_specs=[spec(parts)] * 2 * len(pairs),
        out_specs=[spec(parts // 2)] * 2 * len(pairs),
        compiler_params=pltpu.CompilerParams(vmem_limit_bytes=VMEM_LIMIT),
        cost_estimate=cost(LONG),
        name="pair_sums",
    )(*[array for pair in pairs for array in pair])
    return [outs[2 * i : 2 * i + 2] for i in range(len(pairs))]


def finish_kernel(a_kept, a_got, b_kept, b_got, *refs):
    a_out, b_out = refs[-2:]
    a_out[...] = a_kept[0].astype(f32) + a_got[0].astype(f32)
    b_out[...] = b_kept[0].astype(f32) + b_got[0].astype(f32)


def finish_resident_kernel(a_kept, a_got, b_kept, b_got, *refs):
    a_out, b_out = refs[-2:]
    size = a_out.shape[0]
    at = pl.ds(pl.program_id(0) * size, size)
    a_out[...] = a_kept[0, at].astype(f32) + a_got[a_got.shape[0] - 1, at].astype(f32)
    b_out[...] = b_kept[0, at].astype(f32) + b_got[b_got.shape[0] - 1, at].astype(f32)


def finish(a_kept, a_got, b_kept, b_got, outs, first, hidden_dev, resident=False):
    _, terms, blocks, slab, width = a_kept.shape
    step = 2 if terms % 2 == 0 else 1
    spec = lambda array: pl.BlockSpec(
        (1, terms // step, blocks, slab, width), lambda i, row=array.shape[0] - 1: (row, i, 0, 0, 0)
    )
    out_spec = pl.BlockSpec((terms // step, blocks, slab, width), lambda i: (i, first // blocks, 0, 0))
    shape = jax.ShapeDtypeStruct((terms, hidden_dev, slab, width), f32)
    extra = [] if outs is None else list(outs)
    return pl.pallas_call(
        finish_resident_kernel if resident else finish_kernel,
        out_shape=[shape, shape],
        grid=(step,),
        in_specs=[
            pl.BlockSpec(memory_space=pltpu.VMEM) if resident else spec(array) for array in (a_kept, a_got, b_kept, b_got)
        ]
        + [ANY] * len(extra),
        out_specs=[out_spec] * 2,
        input_output_aliases={4 + i: i for i in range(len(extra))},
        compiler_params=pltpu.CompilerParams(vmem_limit_bytes=VMEM_LIMIT // 2 if resident else VMEM_LIMIT),
        cost_estimate=cost(),
        name="finish",
    )(a_kept, a_got, b_kept, b_got, *extra)


def pause_kernel(_, out_ref):
    out_ref[...] = jnp.zeros(out_ref.shape, f32)


def pause(behind):
    return pl.pallas_call(
        pause_kernel,
        out_shape=jax.ShapeDtypeStruct((8, 128), f32),
        in_specs=[ANY],
        cost_estimate=cost(LONG),
        name="pause",
    )(behind)


def combine_kernel(*refs, blocks_dev, remote_bits, local_bits):
    homes, refs = refs[:blocks_dev], refs[blocks_dev:]
    aways, (mixed_ref, grad_ref) = refs[:-2], refs[-2:]
    width = homes[0].shape[-1]
    for j in range(blocks_dev):
        for side, target in ((0, mixed_ref), (1, grad_ref)):
            total = homes[j][side, 0].astype(f32)
            for bit in range(local_bits):
                total = total + homes[j ^ 1 << bit][side, 1 + bit].astype(f32)
            for bit in range(remote_bits):
                total = total + aways[j * remote_bits + bit][side].astype(f32)
            target[:, j * width : (j + 1) * width] = total.astype(bf16)


def combine(homes, aways, together):
    rows, width = homes[0].shape[-2:]
    blocks_dev = len(homes)
    local_bits, remote_bits = homes[0].shape[1] - 1, len(aways[0])
    chunk = min(rows, 128)
    home = pl.BlockSpec((2, 1 + local_bits, chunk, width), lambda i: (0, 0, i, 0))
    away = [
        pl.BlockSpec((2, chunk, width), lambda i, at=j % together: (at, i, 0))
        for j in range(blocks_dev)
        for _ in range(remote_bits)
    ]
    out = pl.BlockSpec((chunk, blocks_dev * width), lambda i: (i, 0))
    shape = jax.ShapeDtypeStruct((rows, blocks_dev * width), bf16)
    return pl.pallas_call(
        functools.partial(combine_kernel, remote_bits=remote_bits, local_bits=local_bits, blocks_dev=blocks_dev),
        out_shape=[shape, shape],
        grid=(rows // chunk,),
        in_specs=[home] * blocks_dev + away,
        out_specs=[out, out],
        compiler_params=pltpu.CompilerParams(vmem_limit_bytes=VMEM_LIMIT),
        cost_estimate=cost(),
        name="combine",
    )(*homes, *[part for j in range(blocks_dev) for part in aways[j // together]])


def local(frames, up_factors, down_factors, pattern, level_bits, taps, cotangent):
    rows, local_width = frames.shape
    terms, hidden_dev, width, _ = up_factors.shape
    blocks_dev = local_width // width
    ratio = hidden_dev // blocks_dev
    levels = terms - 1
    local_bits = blocks_dev.bit_length() - 1
    remote_bits = levels - local_bits
    far = list(range(1, remote_bits))
    together = min(2, blocks_dev)
    peers = lax.axis_size("seq")
    stages = peers.bit_length() - 1
    scale = 1.0 / math.sqrt(rows * peers)
    place = lax.axis_index("seq").astype(jnp.int32).reshape(1)

    def fetch(pieces, bits):
        got = {bit: swapped(pieces[bit], "tensor", bit) for bit in reversed(bits)}
        return [got[bit] for bit in bits]

    first = lax.pad(frames[:, :width], jnp.zeros((), frames.dtype), ((0, 16, 0), (0, 0, 0)))
    x_first = fetch({bit: first for bit in far}, far)
    x_near = swapped(frames, "tensor", 0)
    before, behind = halo(cotangent)
    before = after(before, x_near)
    g_block = convolution(cotangent, before, behind, taps, (2, 1, 0), width, 1)
    g_first = fetch({bit: g_block for bit in far}, far)
    g_near_first = swapped(g_block, "tensor", 0)
    grad_mixed, both = prepare(frames, cotangent, after(before, g_block), behind, taps, width)
    g_near = swapped(grad_mixed, "tensor", 0)
    x_away = {0: [(value, (0, 0)) for value in x_first]}
    g_away = {0: [(value, (0, 0)) for value in g_first]}
    guards = [x_first, g_first]

    def fetch_far(pieces, *others):
        arrived = fetch({bit: after(pieces[bit], *[g[i] for g in guards], *others) for i, bit in enumerate(far)}, far)
        guards[:] = [arrived]
        return arrived

    def fetch_block(j, *others):
        arrived = fetch_far({bit: both[j - 1] for bit in far}, *others)
        x_away[j] = [(value, (0, 0)) for value in arrived]
        g_away[j] = [(value, (1, 0)) for value in arrived]

    if blocks_dev > 1:
        fetch_block(1)

    homes, aways, sums = [], [], {}
    merged = stages == 2
    x_got, y_got = {}, {}
    away = None
    made = []

    def give_terms(j, *others):
        nonlocal away
        hidden, grad_pre = made[j]
        home, away = term_sums(
            level_bits, pattern, after(hidden, *others) if others else hidden, grad_pre, up_factors, down_factors,
            j, blocks_dev, together, None if j % together == 0 else away,
        )
        homes.append(home)
        if (j + 1) % together == 0:
            aways.append((away[0], fetch_far(away)))

    for j in range(blocks_dev):
        older = None
        if merged and j >= 2:
            older = (sums[j - 2][0], x_got[j - 2], sums[j - 2][1], y_got[j - 2])
        flips = [0] + [1 << bit for bit in range(local_bits)]
        x = [(frames, (0, j ^ flip)) for flip in flips] + [(x_near, (0, j))] + x_away[j]
        g_near_block = (g_near_first, (0, 0)) if j == 0 else (g_near, (0, j))
        g = [(grad_mixed, (0, j ^ flip)) for flip in flips] + [g_near_block] + g_away[j]
        (up_sent, up_kept, down_sent, down_kept), hidden, grad_pre, last = layer(
            level_bits, pattern, place, x, g, up_factors, down_factors, j, blocks_dev, peers, scale, older
        )
        sums[j] = (up_kept, down_kept)
        if older is not None:
            sums[j - 2] = tuple(last)
        if j > 0:
            up_sent, down_sent = after(up_sent, x_got[j - 1]), after(down_sent, y_got[j - 1])
        x_got[j] = swapped(up_sent, "seq", 0)
        y_got[j] = swapped(down_sent, "seq", stages - 1)
        made.append((hidden, grad_pre))
        if j + 2 < blocks_dev:
            fetch_block(j + 2, pause(hidden) if j == 0 else hidden)
        if j >= 1:
            give_terms(j - 1, hidden)
        if j == blocks_dev - 1:
            give_terms(j)

    def combined(*others):
        groups = []
        for near, rest in aways:
            groups.append([swapped(after(near, *others) if others else near, "tensor", 0)] + rest)
        mixed, grad_frames = combine(homes, groups, together)
        return mixed, grad_frames, *halo(mixed)

    outs = None
    if merged:

        def end(j):
            return (sums[j][0], y_got[j + 2], sums[j][1], x_got[j + 2])

        for j in range(max(blocks_dev - 2, 0), blocks_dev):
            got = [x_got[j], y_got[j]]
            if j == blocks_dev - 1:
                for done in range(blocks_dev - 3):
                    outs = finish(*end(done), outs, done * ratio, hidden_dev)
                homes[0] = after(homes[0], *(outs or []))
                mixed, grad_frames, before, behind = combined(*([sums[j - 1][0]] if j else []))
                got = [after(value, before, behind) for value in got]
            (up_last, up_next), (down_last, down_next) = pair_sums([(sums[j][0], got[0]), (sums[j][1], got[1])], (0, 0))
            if j + 1 < blocks_dev:
                down_next, up_next = after(down_next, x_got[j + 1]), after(up_next, y_got[j + 1])
            x_got[j + 2] = swapped(down_next, "seq", 0)
            y_got[j + 2] = swapped(up_next, "seq", 1)
            sums[j] = (up_last, down_last)
        convolved = convolution(mixed, before, behind, taps, (0, 1, 2), width, blocks_dev)
        for j in range(max(blocks_dev - 3, 0), blocks_dev):
            kept, got, down_kept, down_got = end(j)
            if j == blocks_dev - 2:
                got = after(got, convolved)
            outs = finish(kept, got, down_kept, down_got, outs, j * ratio, hidden_dev, j == blocks_dev - 1)
    else:
        for j in range(blocks_dev):
            got = [x_got[j], y_got[j]]
            kept = list(sums[j])
            orders = (list(range(stages)), list(range(stages))[::-1])
            for stage in range(1, stages):
                at = [sorted(order[stage:]).index(order[stage]) for order in orders]
                halves = pair_sums(list(zip(kept, got)), at)
                for side, order in enumerate(orders):
                    kept[side], sent = halves[side]
                    got[side] = swapped(sent, "seq", order[stage])
            outs = finish(kept[0], got[0], kept[1], got[1], outs, j * ratio, hidden_dev)
        mixed, grad_frames, before, behind = combined()
        convolved = convolution(mixed, before, behind, taps, (0, 1, 2), width, blocks_dev)
    return convolved, grad_frames, outs[0], outs[1]


def solution(mesh):
    in_specs = (
        P("seq", "tensor"),
        P(None, "tensor", None, None),
        P(None, "tensor", None, None),
        P("tensor", None),
        P(),
        P(None, "tensor"),
        P("seq", "tensor"),
    )
    out_specs = (
        P("seq", "tensor"),
        P("seq", "tensor"),
        P(None, "tensor", "seq", None),
        P(None, "tensor", "seq", None),
    )
    return jax.shard_map(local, mesh=mesh, in_specs=in_specs, out_specs=out_specs, check_vma=False)
```
